512 devices in a mesh: rep: 64 (over z_lo, y, core), tp: 8 (over x, z_hi).
Axes of the slice: x: 4, y: 8, z: 8 (z_hi: 2, z_lo: 4; z = z_hi * 4 + z_lo), core: 2. Of those that a mesh axis runs over, the one named last changes fastest.
Arguments:
- activations: bfloat16 [64, 1024, 256], P('rep', 'tp'), may hold values from -6 to 6
- out_grads: bfloat16 [64, 1024, 4096], P('rep', None, 'tp'), may hold values from -6 to 6
- weight: bfloat16 [64, 256, 4096], P('rep', None, 'tp'), may hold values from -6 to 6
- public: bfloat16 [64, 256, 4096], P('rep', None, 'tp'), may hold values from -6 to 6
- counts: int32 [64], P('rep'), may hold values from 256 to 1024, as said below
- kept: int32 [64, 8, 40], P('rep', 'tp'), may hold values from 0 to 63, as said below
- distances: int32 [2], replicated, may hold values from 1 to 32, as said below
Outputs:
- new_weight: bfloat16 [64, 256, 4096], P('rep', None, 'tp')
The draws below stay inside these ranges and needn't reach their ends.
Inputs may be any that keep to these rules, and one draw needn't show every extreme that they name: `counts`: at least 256; some replica has exactly 1024. `kept`: the 40 indices of each replica and shard are distinct. `distances`: powers of two, the same for every replica; the rounds' distances differ, and one of the rounds has distance half the number of replicas.
All inputs are finite; a program needn't handle non-finite values.
Results may differ from the reference program's by a relative error of at most 0.006.
Values may be sent and summed in bfloat16 or wider, within the bound.
No kernel may reach another device: no remote copies, remote signals or barrier semaphores. Data moves between devices by JAX's collectives and lax.ppermute only.
A program may use at most 128 MiB of HBM per device.

```python
import jax
import jax.numpy as jnp
from jax import lax

D_WIN = 256
FF_DEV = 512
TOK = 1024
KEEP = 40
ROUNDS = 2
FF_WIN = 4096
N_REP = 64
N_TP = 8


def draw_counts(key, part):
    key = jax.random.fold_in(key, 1)
    key_values, key_place = jax.random.split(key)
    values = jax.random.randint(key_values, (N_REP,), TOK // 4, TOK + 1)
    slot_index = jax.random.randint(key_place, (), 0, N_REP)
    return values.at[slot_index].set(TOK).astype(jnp.int32)


def draw_kept(key, part):
    key = jax.random.fold_in(key, 2)
    subkeys = jax.random.split(key, N_REP * N_TP)
    orders = jax.vmap(lambda single_key: jax.random.permutation(single_key, 64))(subkeys)
    return orders[:, :KEEP].reshape(N_REP, N_TP, KEEP).astype(jnp.int32)


def draw_distances(key, part):
    key = jax.random.fold_in(key, 3)
    key_place, key_other = jax.random.split(key)
    levels = N_REP.bit_length() - 1
    place = jax.random.randint(key_place, (), 0, ROUNDS)
    other = jax.random.randint(key_other, (), 0, levels - 1)
    exponents = jnp.where(jnp.arange(ROUNDS, dtype=jnp.int32) == place, levels - 1, other).astype(jnp.int32)
    return jnp.left_shift(jnp.int32(1), exponents).astype(jnp.int32)


def shard_levels(key, dims, pieces, smallest, high):
    gain = 1.0
    for position, blocks in pieces:
        draws = jax.random.uniform(jax.random.fold_in(jax.random.fold_in(key, 6), position), (blocks,), jnp.float32, smallest / len(pieces), high / len(pieces))
        gain = gain * jnp.repeat(jnp.exp(draws), dims[position] // blocks).reshape((-1,) + (1,) * (len(dims) - 1 - position))
    return gain


def normal_values(stream_key, extent, scale, bound, cuts=(), kind=jnp.bfloat16):
    entries = jax.random.normal(stream_key, extent, jnp.float32) * scale
    if len(cuts) > 0:
        entries = shard_levels(stream_key, extent, cuts, -0.22, 0.18) * entries
    return jnp.clip(entries, min=-bound, max=bound).astype(kind)


def setup_inputs(seed: int = 0) -> dict:
    arg_keys = jax.random.split(jax.random.key(seed), 8)
    activations = normal_values(arg_keys[0], (N_REP, TOK, D_WIN), 1.0, 6.0, ((0, 64), (1, 8)))
    out_grads = normal_values(arg_keys[1], (N_REP, TOK, FF_WIN), 1.0, 6.0, ((0, 64), (2, 8)))
    weight = normal_values(arg_keys[2], (N_REP, D_WIN, FF_WIN), 1.0, 6.0, ((0, 64), (2, 8)))
    public = normal_values(arg_keys[3], (N_REP, D_WIN, FF_WIN), 1.0, 6.0, ((0, 64), (2, 8)))
    counts = draw_counts(jax.random.fold_in(arg_keys[7], 71), 0)
    kept = draw_kept(jax.random.fold_in(arg_keys[7], 71), 0)
    distances = draw_distances(jax.random.fold_in(arg_keys[7], 71), 0)
    return dict(activations=activations, out_grads=out_grads, weight=weight, public=public, counts=counts, kept=kept, distances=distances)


learn_rate = 0.02
mix_weight = 0.5
highest = lax.Precision.HIGHEST

def cosine_table():
    freqs = jnp.arange(64, dtype=jnp.float32)[:, None]
    places = jnp.arange(64, dtype=jnp.float32)[None, :]
    scales = jnp.where(freqs == 0.0, jnp.sqrt(jnp.float32(1.0 / 64.0)), jnp.sqrt(jnp.float32(2.0 / 64.0)))
    return (scales * jnp.cos(jnp.pi * (2.0 * places + 1.0) * freqs / 128.0)).astype(jnp.float32)

def block_index():
    row_blocks = jnp.arange(64, dtype=jnp.int32)[:, None] // 8
    col_blocks = jnp.arange(64, dtype=jnp.int32)[None, :] // 8
    return row_blocks * 8 + col_blocks

def compress(residual, kept_rows):
    table = cosine_table()
    chosen = jnp.any(kept_rows[:, :, None, None] == block_index()[None, None], axis=1).astype(jnp.float32)
    tiles = residual.reshape(D_WIN // 64, 64, N_TP, FF_DEV // 64, 64)
    coeffs = jnp.einsum('un,anbcm,vm->aubcv', table, tiles, table, precision=highest)
    coeffs = coeffs * jnp.transpose(chosen, (1, 0, 2))[None, :, :, None, :]
    restored = jnp.einsum('un,aubcv,vm->anbcm', table, coeffs, table, precision=highest)
    return restored.reshape(D_WIN, FF_WIN)

def replica_grad(operands):
    inputs, cotangents, token_count = operands
    live_rows = (jnp.arange(TOK, dtype=jnp.int32) < token_count).astype(jnp.bfloat16)
    masked = cotangents * live_rows[:, None]
    return lax.dot_general(inputs, masked, (((0,), (0,)), ((), ())), preferred_element_type=jnp.float32)

def compress_pair(operands):
    return compress(operands[0], operands[1])

def reference(activations, out_grads, weight, public, counts, kept, distances):
    gradient = lax.map(replica_grad, (activations, out_grads, counts))
    weights_now = weight.astype(jnp.float32) - learn_rate * gradient
    public_now = public.astype(jnp.float32)
    replica_ids = jnp.arange(N_REP, dtype=jnp.int32)
    for round_index in range(ROUNDS):
        update_own = lax.map(compress_pair, (weights_now - public_now, kept))
        public_now = public_now + update_own
        partners = jnp.bitwise_xor(replica_ids, distances[round_index]).astype(jnp.int32)
        peer_copy = jnp.take(public_now, partners, axis=0)
        weights_now = weights_now + mix_weight * 0.5 * (peer_copy - public_now)
    return weights_now.astype(jnp.bfloat16)
```

```python
import jax
import jax.numpy as jnp
from jax import lax
from jax.sharding import PartitionSpec as P

ROUNDS = 2


learn_rate = 0.02
mix_weight = 0.5
highest = lax.Precision.HIGHEST


def for_sending(x):

    def short(part):
        return part.astype(jnp.bfloat16) if part.dtype == jnp.float32 else part

    return jax.tree.map(short, x)


def swapped(block, axis, apart):
    count = lax.axis_size(axis)
    route = []
    for low in range(count):
        high = low | 1 << apart
        if high != low and high < count:
            route += [(low, high), (high, low)]
    return lax.ppermute(block, axis, route)


def gathered(block):
    count = lax.axis_size("tp")
    copies = jnp.broadcast_to(block[None], (count,) + block.shape)
    return lax.all_to_all(copies, "tp", 0, 0).reshape(-1, block.shape[1])


def cosine_table():
    freqs = jnp.arange(64, dtype=jnp.float32)[:, None]
    places = jnp.arange(64, dtype=jnp.float32)[None, :]
    scales = jnp.where(
        freqs == 0.0, jnp.sqrt(jnp.float32(1.0 / 64.0)), jnp.sqrt(jnp.float32(2.0 / 64.0))
    )
    return scales * jnp.cos(jnp.pi * (2.0 * places + 1.0) * freqs / 128.0)


def transform_forward(residual, table, paired):
    rows_total, cols_total = residual.shape
    stacked = residual.reshape(rows_total // 64, 64, cols_total)
    left_side = jnp.einsum("un,anc->auc", table, stacked, precision=highest)
    right_side = jnp.dot(left_side.reshape(-1, 128), paired.T, precision=highest)
    return right_side.reshape(rows_total // 64, 64, cols_total)


def transform_inverse(coeffs, table, paired):
    tile_rows, sixty_four, cols_total = coeffs.shape
    left_side = jnp.einsum("un,auc->anc", table, coeffs, precision=highest)
    right_side = jnp.dot(left_side.reshape(-1, 128), paired, precision=highest)
    return right_side.reshape(tile_rows * 64, cols_total)


def swap_copies(operand, bit_index, levels):

    def make_swap(level_bit):
        return lambda tiles_in: jax.tree.map(
            lambda part, own: part.astype(own.dtype),
            swapped(for_sending(tiles_in), "rep", level_bit),
            tiles_in,
        )

    return lax.switch(bit_index, [make_swap(level_bit) for level_bit in range(levels)], operand)


def shards(activations, out_grads, weight, public, counts, kept, distances):
    levels = lax.axis_size("rep").bit_length() - 1
    bit_indices = lax.population_count(distances - 1)
    cols_local = weight.shape[2]
    table = cosine_table()
    paired = jnp.kron(jnp.eye(2, dtype=jnp.float32), table)
    kept_local = kept[0, 0]
    row_blocks = jnp.arange(64, dtype=jnp.int32)[:, None] // 8
    col_blocks = jnp.arange(cols_local, dtype=jnp.int32)[None, :] % 64 // 8
    index_grid = row_blocks * 8 + col_blocks
    keep_mask = jnp.any(kept_local[:, None, None] == index_grid[None], axis=0).astype(jnp.float32)
    token_count = counts[0]
    total_tokens = out_grads.shape[1]
    live_rows = (jnp.arange(total_tokens, dtype=jnp.int32) < token_count).astype(jnp.bfloat16)
    grads_live = out_grads[0] * live_rows[:, None]
    gradient = lax.dot_general(
        gathered(activations[0]),
        grads_live,
        (((0,), (0,)), ((), ())),
        preferred_element_type=jnp.float32,
    )
    weights_now = weight[0].astype(jnp.float32) - learn_rate * gradient
    public_now = public[0].astype(jnp.float32)
    for round_index in range(ROUNDS):
        bit_index = bit_indices[round_index]
        coeffs = transform_forward(weights_now - public_now, table, paired) * keep_mask[None]
        update_own = transform_inverse(coeffs, table, paired)
        public_now = public_now + update_own
        peer_copy = swap_copies(public_now, bit_index, levels)
        weights_now = weights_now + mix_weight * 0.5 * (peer_copy - public_now)
    return weights_now.astype(jnp.bfloat16)[None]


def solution(mesh):
    return jax.shard_map(
        shards,
        mesh=mesh,
        in_specs=(
            P("rep", "tp", None),
            P("rep", None, "tp"),
            P("rep", None, "tp"),
            P("rep", None, "tp"),
            P("rep"),
            P("rep", "tp", None),
            P(),
        ),
        out_specs=P("rep", None, "tp"),
        check_vma=False,
    )
```

```python
import jax
import jax.numpy as jnp
import numpy as np
from jax import lax
from jax.experimental import pallas as pl
from jax.experimental.pallas import tpu as pltpu
from jax.sharding import PartitionSpec as P


learn_rate = 0.02
step = 0.25
ROWS, COLS, KEEP, SLABS = 256, 512, 40, 64
LEFT = SLABS - KEEP
f32, bf16, i32 = jnp.float32, jnp.bfloat16, jnp.int32
VM = pl.BlockSpec(memory_space=pltpu.VMEM)
SM = pl.BlockSpec(memory_space=pltpu.SMEM)


def tables():
    u, n = np.arange(64)[:, None], np.arange(64)[None, :]
    table = np.where(u == 0, np.sqrt(1 / 64), np.sqrt(2 / 64)) * np.cos(np.pi * (2 * n + 1) * u / 128)
    left = np.zeros((2, 8, 2, 8, 4, 64))
    for a in range(4):
        left[a // 2, :, a % 2, :, a, :] = table.reshape(8, 8, 64)
    left = left.reshape(ROWS, ROWS)
    right = np.zeros((8, 64, 8, 8, 8))
    for b in range(8):
        right[b, :, :, b, :] = table.T.reshape(64, 8, 8)
    right = right.reshape(COLS, COLS)

    def two(x):
        high = x.astype(jnp.bfloat16)
        return np.stack([high, (x - high.astype(np.float64)).astype(jnp.bfloat16)])

    return two(left), two(left.T), two(right), two(right.T)


def dot(a, b):
    return jnp.dot(a, b, preferred_element_type=f32)


def split(x):
    high = x.astype(bf16)
    return high, (x - high.astype(f32)).astype(bf16)


def left_dot(table, x):
    high, low = split(x)
    return dot(table[0], high) + (dot(table[0], low) + dot(table[1], high))


def right_dot(x, table):
    high, low = split(x)
    return dot(high, table[0]) + (dot(low, table[0]) + dot(high, table[1]))


def low_lanes():
    return lax.broadcasted_iota(i32, (128, 128), 1) < 64


def to_slabs(grid, put):
    low = low_lanes()
    for q in range(4):
        top = grid[:128, 128 * q : 128 * (q + 1)]
        bottom = grid[128:, 128 * q : 128 * (q + 1)]
        even = jnp.where(low, top, pltpu.roll(bottom, 64, 1))
        odd = jnp.where(low, pltpu.roll(top, 64, 1), bottom)
        for ub in range(8):
            put(ub * 8 + 2 * q, even[16 * ub : 16 * (ub + 1)])
            put(ub * 8 + 2 * q + 1, odd[16 * ub : 16 * (ub + 1)])


def from_slabs(get):
    low = low_lanes()
    tops, bottoms = [], []
    for q in range(4):
        even = jnp.concatenate([get(ub * 8 + 2 * q) for ub in range(8)], 0)
        odd = jnp.concatenate([get(ub * 8 + 2 * q + 1) for ub in range(8)], 0)
        tops.append(jnp.where(low, even, pltpu.roll(odd, 64, 1)))
        bottoms.append(jnp.where(low, pltpu.roll(even, 64, 1), odd))
    return jnp.concatenate([jnp.concatenate(tops, 1), jnp.concatenate(bottoms, 1)], 0)


def list_left(kept, rest):
    low, high = jnp.int32(0), jnp.int32(0)
    for i in range(KEEP):
        s = kept[i]
        bit = lax.shift_left(jnp.int32(1), s & 31)
        low = low | jnp.where(s < 32, bit, 0)
        high = high | jnp.where(s < 32, 0, bit)
    count = jnp.int32(0)
    for s in range(SLABS):
        rest[count] = s
        word = low if s < 32 else high
        count = count + 1 - (lax.shift_right_logical(word, jnp.int32(s & 31)) & 1)


def public_kernel(kept, public, kept_row, left, right, coeffs, early, rest):
    x = public[...]
    grid = left_dot(left, dot(x, right[0]) + dot(x, right[1]))

    def put(s, slab):
        coeffs[s] = slab

    to_slabs(grid, put)
    list_left(kept, rest)
    for j in range(LEFT):
        early[j] = coeffs[rest[j]].astype(bf16)
    early[LEFT] = kept_row[...]


def grads_kernel(count, place, grads, weight, left, right, turned, coeffs):
    def block(k, c):
        x = grads[pl.ds(pl.multiple_of(k * 256, 256), 256), :]
        y = dot(x, right[0]) + dot(x, right[1])
        token = k * 256 + lax.broadcasted_iota(i32, (256, COLS), 0)
        y = jnp.where(token < count[0], y, 0.0).astype(bf16)
        for z in range(2):
            to = k * 256 + lax.rem(z + place[0], 2) * 128
            turned[pl.ds(pl.multiple_of(to, 128), 128), :] = y[128 * z : 128 * (z + 1)]
        return c

    lax.fori_loop(0, grads.shape[0] // 256, block, 0)
    x = weight[...]
    coeffs[...] = left_dot(left, dot(x, right[0]) + dot(x, right[1]))


def weights_kernel(kept, acts, turned, weight_coeffs, left, after, late, kept_coeffs, moved, slabs):
    dims = (((1,), (1,)), ((), ()))
    x = acts[...].reshape(-1, ROWS)
    rows = lax.dot_general(left[0], x, dims, preferred_element_type=f32)
    rows += lax.dot_general(left[1], x, dims, preferred_element_type=f32)
    change = -learn_rate * dot(rows.astype(bf16), turned[...])
    moved[...] = change

    def put(s, slab):
        slabs[s] = slab

    to_slabs(weight_coeffs[...] + change, put)
    for i in range(KEEP):
        slab = slabs[kept[i]]
        kept_coeffs[i] = slab
        late[i] = slab.astype(bf16)


def fill_kernel(kept_peer, early, peer, rest):
    list_left(kept_peer, rest)
    for j in range(LEFT):
        peer[rest[j]] = early[j]
    for i in range(KEEP):
        peer[kept_peer[i]] = jnp.zeros((16, 128), bf16)


def first_kernel(kept, kept_peer, arrived, filled, kept_coeffs, late, next_coeffs, peer):
    peer[...] = filled[...]
    for i in range(KEEP):
        peer[kept_peer[i]] = arrived[i]
    for i in range(KEEP):
        value = kept_coeffs[i]
        value = value + step * (peer[kept[i]].astype(f32) - value)
        next_coeffs[i] = value
        late[i] = value.astype(bf16)


def base_kernel(kept, kept_peer, peer, early, coeffs, kept_coeffs, next_coeffs, moved, weight, left_t, right_t, out, delta, rest):
    list_left(kept_peer, rest)
    delta[...] = step * peer[...].astype(f32) - 2 * step * coeffs[...]
    for i in range(KEEP):
        s = kept[i]
        delta[s] = step * (peer[s].astype(f32) - kept_coeffs[i] - next_coeffs[i])
    for j in range(LEFT):
        s = rest[j]
        delta[s] = delta[s] + step * early[j].astype(f32)
    grid = from_slabs(lambda s: delta[s]) + moved[...]
    out[...] = weight[...].astype(f32) + left_dot(left_t, right_dot(grid, right_t))


def last_kernel(kept_peer, arrived, base, left_t, right_t, out, slabs):
    slabs[...] = jnp.zeros(slabs.shape, f32)

    for i in range(KEEP):
        slabs[kept_peer[i]] = step * arrived[i].astype(f32)
    grid = from_slabs(lambda s: slabs[s]).astype(bf16)
    change = dot(left_t[0], dot(grid, right_t[0]).astype(bf16))
    out[...] = (base[...] + change).astype(bf16)


def call(kernel, outs, specs, scratch=(), flops=0, moves=0):
    return pl.pallas_call(
        kernel,
        out_shape=[jax.ShapeDtypeStruct(shape, kind) for shape, kind in outs],
        in_specs=specs,
        out_specs=[VM] * len(outs),
        scratch_shapes=list(scratch),
        compiler_params=pltpu.CompilerParams(vmem_limit_bytes=32 * 2**20),
        cost_estimate=pl.CostEstimate(flops=flops, bytes_accessed=moves, transcendentals=0),
    )


SLAB32 = ((SLABS, 16, 128), f32)
SLAB16 = ((SLABS, 16, 128), bf16)
KEPT32 = ((KEEP, 16, 128), f32)
KEPT16 = ((KEEP, 16, 128), bf16)
GRID32 = ((ROWS, COLS), f32)
ANY = pl.BlockSpec(memory_space=pl.ANY)
REST = pltpu.SMEM((SLABS + 1,), i32)
ROOM = pltpu.VMEM((SLABS, 16, 128), f32)


def do_public(kept, public, kept_row, left, right):
    outs = [SLAB32, ((LEFT + 1, 16, 128), bf16)]
    return call(public_kernel, outs, [SM] + [VM] * 4, [REST], 10**9, 2**21)(kept, public, kept_row, left, right)


def do_grads(count, place, grads, weight, left, right):
    outs = [(grads.shape, bf16), GRID32]
    return call(grads_kernel, outs, [SM, SM] + [VM] * 4, (), 2 * 10**9, 2**22)(count, place, grads, weight, left, right)


def do_weights(kept, acts, turned, weight_coeffs, left, after):
    outs = [KEPT16, KEPT32, GRID32]
    return call(weights_kernel, outs, [SM] + [VM] * 4 + [ANY], [ROOM], 3 * 10**8, 2**21)(kept, acts, turned, weight_coeffs, left, after)


def do_fill(kept_peer, early):
    return call(fill_kernel, [SLAB16], [SM, VM], [REST], 10**6, 2**18)(kept_peer, early)[0]


def do_first(kept, kept_peer, arrived, filled, kept_coeffs):
    return call(first_kernel, [KEPT16, KEPT32, SLAB16], [SM, SM] + [VM] * 3, (), 10**6, 2**19)(kept, kept_peer, arrived, filled, kept_coeffs)


def do_base(kept, kept_peer, *rest):
    return call(base_kernel, [GRID32], [SM, SM] + [VM] * 9, [ROOM, REST], 10**9, 2**22)(kept, kept_peer, *rest)[0]


def do_last(kept_peer, arrived, base, left_t, right_t):
    outs = [((ROWS, COLS), bf16)]
    return call(last_kernel, outs, [SM] + [VM] * 4, [ROOM], 2 * 10**8, 2**20)(kept_peer, arrived, base, left_t, right_t)[0]


def swapped(block, axis, bit):
    count = lax.axis_size(axis)
    return lax.ppermute(block, axis, [(i, i ^ (1 << bit)) for i in range(count)])


def peers_list(early):
    return early[LEFT, 0, :KEEP].astype(i32)


def window(bits, pair, turned, weight_coeffs, weight, public, kept, left, left_t, right, right_t):
    count_x = lax.axis_size("tp") // 2
    groups = [[2 * x + z for x in range(count_x)] for z in range(2)]
    kept_row = jnp.pad(kept.astype(bf16)[None], ((0, 15), (0, 128 - KEEP)))
    acts = lax.all_to_all(jnp.broadcast_to(pair[None], (count_x,) + pair.shape), "tp", 0, 0, axis_index_groups=groups)
    coeffs, early = do_public(kept, public, kept_row, left, right)
    early_first = swapped(early, "rep", bits[0])
    late, kept_coeffs, moved = do_weights(kept, acts, turned, weight_coeffs, left, early)
    arrived = swapped(late, "rep", bits[0])
    early, late = lax.optimization_barrier((early, late))
    early_second = swapped(early, "rep", bits[1])
    kept_first, kept_second = peers_list(early_first), peers_list(early_second)
    filled = do_fill(kept_first, early_first)
    late, next_coeffs, peer = do_first(kept, kept_first, arrived, filled, kept_coeffs)
    arrived = swapped(late, "rep", bits[1])
    base = do_base(kept, kept_second, peer, early_second, coeffs, kept_coeffs, next_coeffs, moved, weight, left_t, right_t)
    return do_last(kept_second, arrived, base, left_t, right_t)


def shards(activations, out_grads, weight, public, counts, kept, distances):
    acts = activations[0]
    other = swapped(acts, "tp", 0)
    top = lax.axis_size("rep").bit_length() - 2
    bits = lax.population_count(distances - 1)
    choice = jnp.where(bits[1] == top, bits[0], top + bits[1])
    ways = [(k, top) for k in range(top)] + [(top, k) for k in range(top)]
    place = (lax.axis_index("tp") % 2).astype(i32)[None]
    left, left_t, right, right_t = (jnp.asarray(t) for t in tables())
    turned, weight_coeffs = do_grads(counts, place, out_grads[0], weight[0], left, right)
    operands = (jnp.stack([acts, other]), turned, weight_coeffs, weight[0], public[0], kept[0, 0], left, left_t, right, right_t)
    branches = [lambda *args, way=way: window(way, *args) for way in ways]
    return lax.switch(choice, branches, *operands)[None]


def solution(mesh):
    return jax.shard_map(
        shards,
        mesh=mesh,
        in_specs=(
            P("rep", "tp", None),
            P("rep", None, "tp"),
            P("rep", None, "tp"),
            P("rep", None, "tp"),
            P("rep"),
            P("rep", "tp", None),
            P(),
        ),
        out_specs=P("rep", None, "tp"),
        check_vma=False,
    )
```

```python
import jax
import jax.numpy as jnp
import numpy as np
from jax import lax
from jax.experimental import pallas as pl
from jax.experimental.pallas import tpu as pltpu
from jax.sharding import PartitionSpec as P


learn_rate = 0.02
step = 0.25
ROWS, COLS, KEEP, SLABS = 256, 512, 40, 64
LEFT = SLABS - KEEP
f32, bf16, i32 = jnp.float32, jnp.bfloat16, jnp.int32
VM = pl.BlockSpec(memory_space=pltpu.VMEM)
SM = pl.BlockSpec(memory_space=pltpu.SMEM)


def cosines(freq, place):
    phase = ((2 * place + 1) * freq) & 255
    scale = jnp.where(freq == 0, np.float32(np.sqrt(1 / 64)), np.float32(np.sqrt(2 / 64)))
    return scale * jnp.cos(phase.astype(f32) * np.float32(np.pi / 128))


def lines(shape, axis):
    return lax.broadcasted_iota(i32, shape, axis)


def row_freq(r):
    return ((r >> 4) & 7) * 8 + (r & 7)


def row_tile(r):
    return 2 * (r >> 7) + ((r >> 3) & 1)


def col_freq(j):
    return (j >> 6) * 8 + (j & 7)


def col_tile(j):
    return (j >> 3) & 7


def left_table():
    shape = (ROWS, 128)
    part = cosines(row_freq(lines(shape, 0)), lines(shape, 1) & 63)
    shape = (ROWS, ROWS)
    return jnp.where(row_tile(lines(shape, 0)) == lines(shape, 1) >> 6, jnp.concatenate([part] * 2, 1), 0.0)


def left_table_t():
    shape = (64, ROWS)
    part = cosines(row_freq(lines(shape, 1)), lines(shape, 0))
    shape = (ROWS, ROWS)
    return jnp.where(row_tile(lines(shape, 1)) == lines(shape, 0) >> 6, jnp.concatenate([part] * 4, 0), 0.0)


def right_table():
    shape = (64, COLS)
    part = cosines(col_freq(lines(shape, 1)), lines(shape, 0))
    shape = (COLS, COLS)
    return jnp.where(col_tile(lines(shape, 1)) == lines(shape, 0) >> 6, jnp.concatenate([part] * 8, 0), 0.0)


def right_table_t():
    shape = (COLS, 128)
    part = cosines(col_freq(lines(shape, 0)), lines(shape, 1) & 63)
    shape = (COLS, COLS)
    return jnp.where(col_tile(lines(shape, 0)) == lines(shape, 1) >> 6, jnp.concatenate([part] * 4, 1), 0.0)


def dot(a, b):
    return jnp.dot(a, b, preferred_element_type=f32)


def split(x):
    high = x.astype(bf16)
    return high, (x - high.astype(f32)).astype(bf16)


def left_dot(table, x):
    high, low = split(x)
    return dot(table[0], high) + (dot(table[0], low) + dot(table[1], high))


def right_dot(x, table):
    high, low = split(x)
    return dot(high, table[0]) + (dot(low, table[0]) + dot(high, table[1]))


def low_lanes():
    return lax.broadcasted_iota(i32, (128, 128), 1) < 64


def to_slabs(grid, put):
    low = low_lanes()
    for q in range(4):
        top = grid[:128, 128 * q : 128 * (q + 1)]
        bottom = grid[128:, 128 * q : 128 * (q + 1)]
        even = jnp.where(low, top, pltpu.roll(bottom, 64, 1))
        odd = jnp.where(low, pltpu.roll(top, 64, 1), bottom)
        for ub in range(8):
            put(ub * 8 + 2 * q, even[16 * ub : 16 * (ub + 1)])
            put(ub * 8 + 2 * q + 1, odd[16 * ub : 16 * (ub + 1)])


def from_slabs(get):
    low = low_lanes()
    tops, bottoms = [], []
    for q in range(4):
        even = jnp.concatenate([get(ub * 8 + 2 * q) for ub in range(8)], 0)
        odd = jnp.concatenate([get(ub * 8 + 2 * q + 1) for ub in range(8)], 0)
        tops.append(jnp.where(low, even, pltpu.roll(odd, 64, 1)))
        bottoms.append(jnp.where(low, pltpu.roll(even, 64, 1), odd))
    return jnp.concatenate([jnp.concatenate(tops, 1), jnp.concatenate(bottoms, 1)], 0)


def list_all(kept, rest):
    lane = lax.broadcasted_iota(i32, (16, 128), 1)
    row = jnp.zeros((16, 128), f32)
    low, high = jnp.int32(0), jnp.int32(0)
    for i in range(KEEP):
        s = kept[i]
        row = jnp.where(lane == i, s.astype(f32), row)
        bit = lax.shift_left(jnp.int32(1), s & 31)
        low = low | jnp.where(s < 32, bit, 0)
        high = high | jnp.where(s < 32, 0, bit)
    count = jnp.int32(0)
    for s in range(SLABS):
        rest[count] = s
        row = jnp.where(lane == count + KEEP, jnp.float32(s), row)
        word = low if s < 32 else high
        count = count + 1 - (lax.shift_right_logical(word, jnp.int32(s & 31)) & 1)
    return row


def public_kernel(kept, public, coeffs, full, early, left_two, right_two, rest):
    left, right = split(left_table()), split(right_table())
    for k in range(2):
        left_two[k] = left[k]
        right_two[k] = right[k]
    x = public[...]
    grid = left_dot(left_two, dot(x, right_two[0]) + dot(x, right_two[1]))

    def put(s, slab):
        coeffs[s] = slab
        full[s] = slab.astype(bf16)

    to_slabs(grid, put)
    row = list_all(kept, rest)
    for j in range(LEFT):
        early[j] = full[rest[j]]
    early[LEFT] = row.astype(bf16)


def spread_kernel(own, other, out):
    for x in range(out.shape[0]):
        out[x, 0] = own[...]
        out[x, 1] = other[...]


def grads_kernel(count, place, way, grads, weight, right, turned, weight_turned):
    part = grads.shape[0] // 4
    for k in range(4):
        y = dot(grads[k * part : (k + 1) * part], right[0])
        token = k * part + lines((part, COLS), 0)
        y = jnp.where(token < count[0], y, 0.0).astype(bf16)
        for z in range(2):
            to = k * part + ((z + place[0]) & 1) * (part // 2)
            turned[pl.ds(pl.multiple_of(to, part // 2), part // 2), :] = y[part // 2 * z : part // 2 * (z + 1)]
    x = weight[...]
    weight_turned[...] = (dot(x, right[0]) + dot(x, right[1])).astype(bf16)


def weights_kernel(kept, acts, turned, weight_turned, left, public_full, packed, full, kept_coeffs, moved, slabs):
    dims = (((1,), (1,)), ((), ()))
    x = acts[...].reshape(-1, ROWS)
    rows = lax.dot_general(left[0], x, dims, preferred_element_type=f32)
    rows += lax.dot_general(left[1], x, dims, preferred_element_type=f32)
    change = -learn_rate * dot(rows.astype(bf16), turned[...])
    moved[...] = change

    def put(s, slab):
        slabs[s] = slab

    x = weight_turned[...]
    to_slabs(dot(left[0], x) + dot(left[1], x) + change, put)
    full[...] = public_full[...]
    for i in range(KEEP):
        s = kept[i]
        slab = slabs[s]
        short = slab.astype(bf16)
        kept_coeffs[i] = slab
        packed[i] = short
        full[s] = short


def fill_kernel(listed, early, peer):
    for j in range(LEFT):
        peer[listed[KEEP + j]] = early[j]
    for i in range(KEEP):
        peer[listed[i]] = jnp.zeros((16, 128), bf16)


def mix(kept, peer, own, kept_coeffs, packed, full, next_coeffs):
    full[...] = own[...]
    for i in range(KEEP):
        s = kept[i]
        value = kept_coeffs[i]
        value = value + step * (peer[s].astype(f32) - value)
        short = value.astype(bf16)
        next_coeffs[i] = value
        packed[i] = short
        full[s] = short


def near_kernel(kept, peer, own, kept_coeffs, packed, full, next_coeffs):
    mix(kept, peer, own, kept_coeffs, packed, full, next_coeffs)


def far_kernel(kept, listed, arrived, filled, own, kept_coeffs, packed, full, next_coeffs, peer):
    peer[...] = filled[...]
    for i in range(KEEP):
        peer[listed[i]] = arrived[i]
    mix(kept, peer, own, kept_coeffs, packed, full, next_coeffs)


def base_kernel(kept, peer, coeffs, kept_coeffs, next_coeffs, moved, weight, out, left_high, right_high, delta):
    delta[...] = step * peer[...].astype(f32) - 2 * step * coeffs[...]
    for i in range(KEEP):
        s = kept[i]
        delta[s] = step * (peer[s].astype(f32) - kept_coeffs[i] - next_coeffs[i])
    grid = from_slabs(lambda s: delta[s]) + moved[...]
    left, right = split(left_table_t()), split(right_table_t())
    left_high[...] = left[0]
    right_high[...] = right[0]
    out[...] = weight[...].astype(f32) + left_dot(left, right_dot(grid, right))


def finish(get, base, left_t, right_t, out):
    grid = (step * from_slabs(lambda s: get(s).astype(f32))).astype(bf16)
    turned = dot(grid, right_t[...]).astype(bf16)
    out[...] = (base[...] + dot(left_t[...], turned)).astype(bf16)


def near_last_kernel(peer, base, left_t, right_t, out):
    finish(lambda s: peer[s], base, left_t, right_t, out)


def far_last_kernel(listed, arrived, filled, base, left_t, right_t, out, slabs):
    slabs[...] = filled[...]
    for i in range(KEEP):
        slabs[listed[i]] = arrived[i]
    finish(lambda s: slabs[s], base, left_t, right_t, out)


def call(kernel, outs, specs, scratch=(), flops=0, moves=0):
    return pl.pallas_call(
        kernel,
        out_shape=[jax.ShapeDtypeStruct(shape, kind) for shape, kind in outs],
        in_specs=specs,
        out_specs=[VM] * len(outs),
        scratch_shapes=list(scratch),
        compiler_params=pltpu.CompilerParams(vmem_limit_bytes=16 * 2**20),
        cost_estimate=pl.CostEstimate(flops=flops, bytes_accessed=moves, transcendentals=0),
    )


SLAB32 = ((SLABS, 16, 128), f32)
SLAB16 = ((SLABS, 16, 128), bf16)
KEPT32 = ((KEEP, 16, 128), f32)
KEPT16 = ((KEEP, 16, 128), bf16)
GRID32 = ((ROWS, COLS), f32)
GRID16 = ((ROWS, COLS), bf16)
REST = pltpu.SMEM((SLABS + 1,), i32)
ROOM32, ROOM16 = pltpu.VMEM((SLABS, 16, 128), f32), pltpu.VMEM((SLABS, 16, 128), bf16)


TWO_LEFT, TWO_RIGHT = ((2, ROWS, ROWS), bf16), ((2, COLS, COLS), bf16)


def do_public(kept, public):
    outs = [SLAB32, SLAB16, ((LEFT + 1, 16, 128), bf16), TWO_LEFT, TWO_RIGHT]
    return call(public_kernel, outs, [SM, VM], [REST], 10**9, 2**21)(kept, public)


def do_spread(count, own, other):
    return call(spread_kernel, [((count, 2) + own.shape, bf16)], [VM, VM], (), 10**5, 2**20)(own, other)[0]


def do_grads(count, place, way, grads, weight, right):
    outs = [(grads.shape, bf16), GRID16]
    return call(grads_kernel, outs, [SM] * 3 + [VM] * 3, (), 2 * 10**9, 2**22)(count, place, way, grads, weight, right)


def do_weights(kept, *rest):
    outs = [KEPT16, SLAB16, KEPT32, GRID32]
    return call(weights_kernel, outs, [SM] + [VM] * 5, [ROOM32], 3 * 10**8, 2**21)(kept, *rest)


def do_fill(listed, early):
    return call(fill_kernel, [SLAB16], [SM, VM], (), 10**6, 2**18)(listed, early)[0]


def do_near(kept, peer, own, kept_coeffs):
    return [*call(near_kernel, [KEPT16, SLAB16, KEPT32], [SM] + [VM] * 3, (), 10**6, 2**19)(kept, peer, own, kept_coeffs), peer]


def do_far(kept, listed, *rest):
    return list(call(far_kernel, [KEPT16, SLAB16, KEPT32, SLAB16], [SM, SM] + [VM] * 4, (), 10**6, 2**19)(kept, listed, *rest))


def do_base(kept, *rest):
    outs = [GRID32, ((ROWS, ROWS), bf16), ((COLS, COLS), bf16)]
    return call(base_kernel, outs, [SM] + [VM] * 6, [ROOM32], 10**9, 2**22)(kept, *rest)


def do_near_last(*args):
    return call(near_last_kernel, [GRID16], [VM] * 4, (), 2 * 10**8, 2**20)(*args)[0]


def do_far_last(listed, *rest):
    return call(far_last_kernel, [GRID16], [SM] + [VM] * 5, [ROOM16], 2 * 10**8, 2**20)(listed, *rest)[0]


def swapped(block, axis, bit):
    count = lax.axis_size(axis)
    return lax.ppermute(block, axis, [(i, i ^ (1 << bit)) for i in range(count)])


def peers_list(early):
    return early[LEFT, 0, :SLABS].astype(i32)


def shards(activations, out_grads, weight, public, counts, kept, distances):
    top = lax.axis_size("rep").bit_length() - 2
    count_x = lax.axis_size("tp") // 2
    groups = [[2 * x + z for x in range(count_x)] for z in range(2)]
    place = (lax.axis_index("tp") & 1).astype(i32)[None]
    acts, grads, weight, public, kept = activations[0], out_grads[0], weight[0], public[0], kept[0, 0]

    bits = lax.population_count(distances - 1)
    way = jnp.sum(jnp.where(bits == top, jnp.array([top, 0], i32), bits))
    ways = [(bit, top) for bit in range(top)] + [(top, bit) for bit in range(top)]
    known = lax.clamp(jnp.int32(0), way, jnp.int32(len(ways) - 1))[None]
    other = swapped(acts, "tp", 0)
    coeffs, public_full, early, left_two, right_two = do_public(kept, public)
    early_far = swapped(early, "rep", top)
    other, public_full = lax.optimization_barrier((other, public_full))
    pairs = do_spread(count_x, acts, other)
    pairs, counts = lax.optimization_barrier((pairs, counts))
    rows = lax.all_to_all(pairs, "tp", 0, 0, axis_index_groups=groups)
    turned, weight_turned = do_grads(counts, place, known, grads, weight, right_two)
    packed, full, kept_coeffs, moved = do_weights(kept, rows, turned, weight_turned, left_two, public_full)

    def rounds(first, second):
        def run(packed, full, early_far):
            listed = peers_list(early_far)
            filled = do_fill(listed, early_far)
            if first == top:
                packed, full, next_coeffs, peer = do_far(kept, listed, swapped(packed, "rep", first), filled, full, kept_coeffs)
            else:
                packed, full, next_coeffs, peer = do_near(kept, swapped(full, "rep", first), full, kept_coeffs)
            arrived = swapped(packed if second == top else full, "rep", second)
            last = do_base(kept, peer, coeffs, kept_coeffs, next_coeffs, moved, weight)
            if second == top:
                return do_far_last(listed, arrived, filled, *last)
            return do_near_last(arrived, *last)

        return run

    return lax.switch(way, [rounds(*pair) for pair in ways], packed, full, early_far)[None]


def solution(mesh):
    return jax.shard_map(
        shards,
        mesh=mesh,
        in_specs=(
            P("rep", "tp", None),
            P("rep", None, "tp"),
            P("rep", None, "tp"),
            P("rep", None, "tp"),
            P("rep"),
            P("rep", "tp", None),
            P(),
        ),
        out_specs=P("rep", None, "tp"),
        check_vma=False,
    )
```

```python
import jax
import jax.numpy as jnp
import numpy as np
from jax import lax
from jax.experimental import pallas as pl
from jax.experimental.pallas import tpu as pltpu
from jax.sharding import PartitionSpec as P


learn_rate = 0.02
step = 0.25
ROWS, COLS, KEEP, SLABS, TOP = 256, 512, 40, 64, 5
LEFT = SLABS - KEEP
f32, bf16, i32 = jnp.float32, jnp.bfloat16, jnp.int32
VM = pl.BlockSpec(memory_space=pltpu.VMEM)
SM = pl.BlockSpec(memory_space=pltpu.SMEM)


def cosines(freq, place):
    phase = ((2 * place + 1) * freq) & 255
    scale = jnp.where(freq == 0, np.float32(np.sqrt(1 / 64)), np.float32(np.sqrt(2 / 64)))
    return scale * jnp.cos(phase.astype(f32) * np.float32(np.pi / 128))


def lines(shape, axis):
    return lax.broadcasted_iota(i32, shape, axis)


def spectrum():
    shape = (64, 128)
    return cosines(lines(shape, 0), lines(shape, 1) & 63)


def left_table(table):
    groups = [table[8 * ub : 8 * ub + 8] for ub in range(8) for _ in range(2)]
    shape = (128, 128)
    return jnp.where((lines(shape, 0) >> 3) & 1 == lines(shape, 1) >> 6, jnp.concatenate(groups, 0), 0.0)


def left_table_t():
    shape = (64, 128)
    r = lines(shape, 1)
    part = cosines((r >> 4) * 8 + (r & 7), lines(shape, 0))
    odd = (r >> 3) & 1
    return jnp.concatenate([jnp.where(odd == 0, part, 0.0), jnp.where(odd == 1, part, 0.0)], 0)


def right_table():
    shape = (64, COLS)
    j = lines(shape, 1)
    part = cosines((j >> 6) * 8 + (j & 7), lines(shape, 0))
    tile = (j >> 3) & 7
    return jnp.concatenate([jnp.where(tile == b, part, 0.0).astype(bf16) for b in range(8)], 0)


def right_table_t():
    table = spectrum()
    low = lines(table.shape, 1) < 64
    masked = jnp.where(low, table, 0.0), jnp.where(low, 0.0, table)
    zeros = jnp.zeros((8, 128), f32)
    columns = []
    for c in range(4):
        groups = [masked[b & 1][8 * vb : 8 * vb + 8] if b >> 1 == c else zeros for vb in range(8) for b in range(8)]
        columns.append(jnp.concatenate(groups, 0))
    return jnp.concatenate(columns, 1)


def dot(a, b):
    return jnp.dot(a, b, preferred_element_type=f32)


def split(x):
    high = x.astype(bf16)
    return high, (x - high.astype(f32)).astype(bf16)


def by_halves(run, x):
    return jnp.concatenate([run(x[:128]), run(x[128:])], 0)


def left_dot(table, x):
    high, low = split(x)
    return dot(table[0], high) + (dot(table[0], low) + dot(table[1], high))


def right_dot(x, table):
    high, low = split(x)
    return dot(high, table[0]) + (dot(low, table[0]) + dot(high, table[1]))


def low_lanes():
    return lax.broadcasted_iota(i32, (128, 128), 1) < 64


def to_slabs(grid, put):
    low = low_lanes()
    for q in range(4):
        top = grid[:128, 128 * q : 128 * (q + 1)]
        bottom = grid[128:, 128 * q : 128 * (q + 1)]
        even = jnp.where(low, top, pltpu.roll(bottom, 64, 1))
        odd = jnp.where(low, pltpu.roll(top, 64, 1), bottom)
        for ub in range(8):
            put(ub * 8 + 2 * q, even[16 * ub : 16 * (ub + 1)])
            put(ub * 8 + 2 * q + 1, odd[16 * ub : 16 * (ub + 1)])


def from_slabs(get):
    low = low_lanes()
    tops, bottoms = [], []
    for q in range(4):
        even = jnp.concatenate([get(ub * 8 + 2 * q) for ub in range(8)], 0)
        odd = jnp.concatenate([get(ub * 8 + 2 * q + 1) for ub in range(8)], 0)
        tops.append(jnp.where(low, even, pltpu.roll(odd, 64, 1)))
        bottoms.append(jnp.where(low, pltpu.roll(even, 64, 1), odd))
    return jnp.concatenate([jnp.concatenate(tops, 1), jnp.concatenate(bottoms, 1)], 0)


def list_all(kept, room):
    room[...] = jnp.full((1, 128), -1, i32)
    room[:, :KEEP] = kept[...]
    named = room[...]
    shape = (SLABS, 128)
    s, lane = lines(shape, 0), lines(shape, 1)
    hits = jnp.where(s == named, 1.0, 0.0)
    free = jnp.broadcast_to(1.0 - jnp.max(hits, axis=1, keepdims=True), shape)
    shape = (SLABS, SLABS)
    below = jnp.where(lines(shape, 1) < lines(shape, 0), 1.0, 0.0)
    rank = dot(below.astype(bf16), free.astype(bf16))
    here = jnp.where((lane - KEEP).astype(f32) == rank, free, 0.0)
    rest = jnp.sum(here * s.astype(f32), axis=0, keepdims=True)
    row = jnp.where(lane[:1] < KEEP, named.astype(f32), rest)
    room[...] = row.astype(i32)
    return row


def find_way(distances, way):
    sizes = [sum((distances[k] > 1 << bit).astype(i32) for bit in range(TOP)) for k in range(2)]
    way[0] = jnp.where(sizes[1] == TOP, sizes[0], TOP + sizes[1])


def public_kernel(distances, kept, public, acts, coeffs, full, early, pairs, way, room, listed, sems, sem):
    count_x = pairs.shape[0]
    copies = [pltpu.make_async_copy(acts, pairs.at[x, 0], sems.at[x]) for x in range(count_x)]
    for copy in copies:
        copy.start()
    find_way(distances, way)
    row = list_all(kept, room)
    to_scalars = pltpu.make_async_copy(room, listed, sem.at[0])
    to_scalars.start()
    left, right = left_table(spectrum()).astype(bf16), right_table()
    grid = by_halves(lambda x: dot(left, x), dot(public[...], right).astype(bf16))

    def put(s, slab):
        coeffs[s] = slab
        full[s] = slab.astype(bf16)

    to_slabs(grid, put)
    early[LEFT] = jnp.broadcast_to(row, (16, 128)).astype(bf16)
    to_scalars.wait()
    for j in range(LEFT):
        early[j] = full[listed[0, KEEP + j]]
    for copy in copies:
        copy.wait()


def spread_kernel(other, pairs, out, sems):
    copies = [pltpu.make_async_copy(other, out.at[x, 1], sems.at[x]) for x in range(out.shape[0])]
    for copy in copies:
        copy.start()
    for copy in copies:
        copy.wait()


def own_place():
    return lax.axis_index("tp") & 1


def grads_kernel(count, grads, weight, turned, weight_turned):
    place = own_place()
    right = right_table()
    part = grads.shape[0] // 4
    for k in range(4):
        y = dot(grads[k * part : (k + 1) * part], right)
        token = k * part + lines((part, COLS), 0)
        y = jnp.where(token < count[...], y, 0.0).astype(bf16)
        for z in range(2):
            to = k * part + ((z + place) & 1) * (part // 2)
            turned[pl.ds(pl.multiple_of(to, part // 2), part // 2), :] = y[part // 2 * z : part // 2 * (z + 1)]
    weight_turned[...] = dot(weight[...], right).astype(bf16)


def weights_kernel(kept, acts, turned, weight_turned, public_full, packed, full, kept_coeffs, moved, slabs):
    left = split(left_table(spectrum()))
    dims = (((1,), (1,)), ((), ()))
    x = acts[...].reshape(-1, ROWS)
    rows = []
    for h in range(2):
        half = x[:, 128 * h : 128 * (h + 1)]
        row = lax.dot_general(left[0], half, dims, preferred_element_type=f32)
        rows.append((row + lax.dot_general(left[1], half, dims, preferred_element_type=f32)).astype(bf16))
    change = -learn_rate * dot(jnp.concatenate(rows, 0), turned[...])
    moved[...] = change

    def put(s, slab):
        slabs[s] = slab

    to_slabs(by_halves(lambda x: dot(left[0], x), weight_turned[...]) + change, put)
    full[...] = public_full[...]
    for i in range(KEEP):
        s = kept[i]
        slab = slabs[s]
        short = slab.astype(bf16)
        kept_coeffs[i] = slab
        packed[i] = short
        full[s] = short


def fill_kernel(listed, early, peer):
    for j in range(LEFT):
        peer[listed[KEEP + j]] = early[j]
    for i in range(KEEP):
        peer[listed[i]] = jnp.zeros((16, 128), bf16)


def mix(kept, peer, own, kept_coeffs, packed, full, next_coeffs):
    full[...] = own[...]
    for i in range(KEEP):
        s = kept[i]
        value = kept_coeffs[i]
        value = value + step * (peer[s].astype(f32) - value)
        short = value.astype(bf16)
        next_coeffs[i] = value
        packed[i] = short
        full[s] = short


def near_kernel(kept, peer, own, kept_coeffs, packed, full, next_coeffs):
    mix(kept, peer, own, kept_coeffs, packed, full, next_coeffs)


def far_kernel(kept, listed, arrived, filled, own, kept_coeffs, packed, full, next_coeffs, peer):
    peer[...] = filled[...]
    for i in range(KEEP):
        peer[listed[i]] = arrived[i]
    mix(kept, peer, own, kept_coeffs, packed, full, next_coeffs)


def base_kernel(kept, peer, coeffs, kept_coeffs, next_coeffs, moved, weight, out, left_high, right_high, delta):
    delta[...] = step * peer[...].astype(f32) - 2 * step * coeffs[...]
    for i in range(KEEP):
        s = kept[i]
        delta[s] = step * (peer[s].astype(f32) - kept_coeffs[i] - next_coeffs[i])
    grid = from_slabs(lambda s: delta[s]) + moved[...]
    left, right = split(left_table_t()), split(right_table_t())
    left_high[...] = left[0]
    right_high[...] = right[0]
    out[...] = weight[...].astype(f32) + by_halves(lambda x: left_dot(left, x), right_dot(grid, right))


def finish(get, base, left_t, right_t, out):
    grid = (step * from_slabs(lambda s: get(s).astype(f32))).astype(bf16)
    turned = dot(grid, right_t[...]).astype(bf16)
    out[...] = (base[...] + by_halves(lambda x: dot(left_t[...], x), turned)).astype(bf16)


def near_last_kernel(peer, base, left_t, right_t, out):
    finish(lambda s: peer[s], base, left_t, right_t, out)


def far_last_kernel(listed, arrived, filled, base, left_t, right_t, out, slabs):
    slabs[...] = filled[...]
    for i in range(KEEP):
        slabs[listed[i]] = arrived[i]
    finish(lambda s: slabs[s], base, left_t, right_t, out)


def call(kernel, outs, specs, scratch=(), flops=0, moves=0, out_specs=None, aliases=None):
    return pl.pallas_call(
        kernel,
        out_shape=[jax.ShapeDtypeStruct(shape, kind) for shape, kind in outs],
        in_specs=specs,
        out_specs=out_specs or [VM] * len(outs),
        scratch_shapes=list(scratch),
        input_output_aliases=aliases or {},
        compiler_params=pltpu.CompilerParams(vmem_limit_bytes=16 * 2**20),
        cost_estimate=pl.CostEstimate(flops=flops, bytes_accessed=moves, transcendentals=0),
    )


SLAB32 = ((SLABS, 16, 128), f32)
SLAB16 = ((SLABS, 16, 128), bf16)
KEPT32 = ((KEEP, 16, 128), f32)
KEPT16 = ((KEEP, 16, 128), bf16)
GRID32 = ((ROWS, COLS), f32)
GRID16 = ((ROWS, COLS), bf16)
REST = pltpu.SMEM((SLABS + 1,), i32)
ROOM32, ROOM16 = pltpu.VMEM((SLABS, 16, 128), f32), pltpu.VMEM((SLABS, 16, 128), bf16)


ANY = pl.BlockSpec(memory_space=pl.ANY)


def sems(count):
    return pltpu.SemaphoreType.DMA((count,))


def do_public(count, distances, kept, public, acts):
    outs = [SLAB32, SLAB16, ((LEFT + 1, 16, 128), bf16), ((count, 2) + acts.shape, bf16), ((1,), i32)]
    scratch = [pltpu.VMEM((1, 128), i32), pltpu.SMEM((1, 128), i32), sems(count), sems(1)]
    return call(public_kernel, outs, [SM, VM, VM, ANY], scratch, 10**9, 2**21, [VM, VM, VM, ANY, SM])(distances, kept, public, acts)


def do_spread(other, pairs):
    outs = [(pairs.shape, bf16)]
    return call(spread_kernel, outs, [VM, ANY], [sems(pairs.shape[0])], 10**5, 2**20, [ANY], {1: 0})(other, pairs)[0]


def do_grads(count, grads, weight):
    return call(grads_kernel, [(grads.shape, bf16), GRID16], [VM] * 3, (), 2 * 10**9, 2**22)(count, grads, weight)


def do_weights(kept, *rest):
    outs = [KEPT16, SLAB16, KEPT32, GRID32]
    return call(weights_kernel, outs, [SM] + [VM] * 4, [ROOM32], 3 * 10**8, 2**21)(kept, *rest)


def do_fill(listed, early):
    return call(fill_kernel, [SLAB16], [SM, VM], (), 10**6, 2**18)(listed, early)[0]


def do_near(kept, peer, own, kept_coeffs):
    return [*call(near_kernel, [KEPT16, SLAB16, KEPT32], [SM] + [VM] * 3, (), 10**6, 2**19)(kept, peer, own, kept_coeffs), peer]


def do_far(kept, listed, *rest):
    return list(call(far_kernel, [KEPT16, SLAB16, KEPT32, SLAB16], [SM, SM] + [VM] * 4, (), 10**6, 2**19)(kept, listed, *rest))


def do_base(kept, *rest):
    outs = [GRID32, ((128, 128), bf16), ((COLS, COLS), bf16)]
    return call(base_kernel, outs, [SM] + [VM] * 6, [ROOM32], 10**9, 2**22)(kept, *rest)


def do_near_last(*args):
    return call(near_last_kernel, [GRID16], [VM] * 4, (), 2 * 10**8, 2**20)(*args)[0]


def do_far_last(listed, *rest):
    return call(far_last_kernel, [GRID16], [SM] + [VM] * 5, [ROOM16], 2 * 10**8, 2**20)(listed, *rest)[0]


def swapped(block, axis, bit):
    count = lax.axis_size(axis)
    return lax.ppermute(block, axis, [(i, i ^ (1 << bit)) for i in range(count)])


def peers_list(early):
    return early[LEFT, 0, :SLABS].astype(i32)


def shards(activations, out_grads, weight, public, counts, kept, distances):
    top = TOP
    count_x = lax.axis_size("tp") // 2
    groups = [[2 * x + z for x in range(count_x)] for z in range(2)]
    acts, grads, weight, public, kept = activations[0], out_grads[0], weight[0], public[0], kept[0, 0]

    other = swapped(acts, "tp", 0)
    coeffs, public_full, early, pairs, way = do_public(count_x, distances, kept[None], public, acts)
    early_far = swapped(early, "rep", top)
    pairs = do_spread(other, pairs)
    pairs, counts = lax.optimization_barrier((pairs, counts[:, None]))
    rows = lax.all_to_all(pairs, "tp", 0, 0, axis_index_groups=groups)
    turned, weight_turned = do_grads(counts, grads, weight)
    packed, full, kept_coeffs, moved = do_weights(kept, rows, turned, weight_turned, public_full)

    def rounds(first, second):
        def run(packed, full, early_far):
            listed = peers_list(early_far)
            filled = do_fill(listed, early_far)
            if first == top:
                packed, full, next_coeffs, peer = do_far(kept, listed, swapped(packed, "rep", first), filled, full, kept_coeffs)
            else:
                packed, full, next_coeffs, peer = do_near(kept, swapped(full, "rep", first), full, kept_coeffs)
            arrived = swapped(packed if second == top else full, "rep", second)
            last = do_base(kept, peer, coeffs, kept_coeffs, next_coeffs, moved, weight)
            if second == top:
                return do_far_last(listed, arrived, filled, *last)
            return do_near_last(arrived, *last)

        return run

    ways = [(bit, top) for bit in range(top)] + [(top, bit) for bit in range(top)]
    return lax.switch(way[0], [rounds(*pair) for pair in ways], packed, full, early_far)[None]


def solution(mesh):
    return jax.shard_map(
        shards,
        mesh=mesh,
        in_specs=(
            P("rep", "tp", None),
            P("rep", None, "tp"),
            P("rep", None, "tp"),
            P("rep", None, "tp"),
            P("rep"),
            P("rep", "tp", None),
            P(),
        ),
        out_specs=P("rep", None, "tp"),
        check_vma=False,
    )
```

```python
import jax
import jax.numpy as jnp
import numpy as np
from jax import lax
from jax.experimental import pallas as pl
from jax.experimental.pallas import tpu as pltpu
from jax.sharding import PartitionSpec as P


learn_rate = 0.02
step = 0.25
ROWS, COLS, KEEP, SLABS, TOP = 256, 512, 40, 64, 5
LEFT = SLABS - KEEP
PACKED = (2, 3, TOP)
f32, bf16, i32 = jnp.float32, jnp.bfloat16, jnp.int32
VM = pl.BlockSpec(memory_space=pltpu.VMEM)
SM = pl.BlockSpec(memory_space=pltpu.SMEM)


def cosines(freq, place):
    phase = ((2 * place + 1) * freq) & 255
    scale = jnp.where(freq == 0, np.float32(np.sqrt(1 / 64)), np.float32(np.sqrt(2 / 64)))
    return scale * jnp.cos(phase.astype(f32) * np.float32(np.pi / 128))


def lines(shape, axis):
    return lax.broadcasted_iota(i32, shape, axis)


def spectrum():
    shape = (64, 128)
    return cosines(lines(shape, 0), lines(shape, 1) & 63)


def left_table(table):
    groups = [table[8 * ub : 8 * ub + 8] for ub in range(8) for _ in range(2)]
    shape = (128, 128)
    return jnp.where((lines(shape, 0) >> 3) & 1 == lines(shape, 1) >> 6, jnp.concatenate(groups, 0), 0.0)


def left_table_t():
    shape = (64, 128)
    r = lines(shape, 1)
    part = cosines((r >> 4) * 8 + (r & 7), lines(shape, 0))
    odd = (r >> 3) & 1
    return jnp.concatenate([jnp.where(odd == 0, part, 0.0), jnp.where(odd == 1, part, 0.0)], 0)


def right_table():
    shape = (64, COLS)
    j = lines(shape, 1)
    part = cosines((j >> 6) * 8 + (j & 7), lines(shape, 0))
    tile = (j >> 3) & 7
    return jnp.concatenate([jnp.where(tile == b, part, 0.0).astype(bf16) for b in range(8)], 0)


def right_table_t():
    table = spectrum()
    low = lines(table.shape, 1) < 64
    masked = jnp.where(low, table, 0.0), jnp.where(low, 0.0, table)
    zeros = jnp.zeros((8, 128), f32)
    columns = []
    for c in range(4):
        groups = [masked[b & 1][8 * vb : 8 * vb + 8] if b >> 1 == c else zeros for vb in range(8) for b in range(8)]
        columns.append(jnp.concatenate(groups, 0))
    return jnp.concatenate(columns, 1)


def dot(a, b):
    return jnp.dot(a, b, preferred_element_type=f32)


def split(x):
    high = x.astype(bf16)
    return high, (x - high.astype(f32)).astype(bf16)


def by_halves(run, x):
    return jnp.concatenate([run(x[:128]), run(x[128:])], 0)


def left_dot(table, x):
    high, low = split(x)
    return dot(table[0], high) + (dot(table[0], low) + dot(table[1], high))


def right_dot(x, table):
    high, low = split(x)
    return dot(high, table[0]) + (dot(low, table[0]) + dot(high, table[1]))


def low_lanes():
    return lax.broadcasted_iota(i32, (128, 128), 1) < 64


def to_slabs(grid, put):
    low = low_lanes()
    for q in range(4):
        top = grid[:128, 128 * q : 128 * (q + 1)]
        bottom = grid[128:, 128 * q : 128 * (q + 1)]
        even = jnp.where(low, top, pltpu.roll(bottom, 64, 1))
        odd = jnp.where(low, pltpu.roll(top, 64, 1), bottom)
        for ub in range(8):
            put(ub * 8 + 2 * q, even[16 * ub : 16 * (ub + 1)])
            put(ub * 8 + 2 * q + 1, odd[16 * ub : 16 * (ub + 1)])


def from_slabs(get):
    low = low_lanes()
    tops, bottoms = [], []
    for q in range(4):
        even = jnp.concatenate([get(ub * 8 + 2 * q) for ub in range(8)], 0)
        odd = jnp.concatenate([get(ub * 8 + 2 * q + 1) for ub in range(8)], 0)
        tops.append(jnp.where(low, even, pltpu.roll(odd, 64, 1)))
        bottoms.append(jnp.where(low, pltpu.roll(even, 64, 1), odd))
    return jnp.concatenate([jnp.concatenate(tops, 1), jnp.concatenate(bottoms, 1)], 0)


def list_all(kept, room):
    room[...] = jnp.full((1, 128), -1, i32)
    room[:, :KEEP] = kept[...]
    named = room[...]
    shape = (SLABS, 128)
    s, lane = lines(shape, 0), lines(shape, 1)
    hits = jnp.where(s == named, 1.0, 0.0)
    free = jnp.broadcast_to(1.0 - jnp.max(hits, axis=1, keepdims=True), shape)
    shape = (SLABS, SLABS)
    below = jnp.where(lines(shape, 1) < lines(shape, 0), 1.0, 0.0)
    rank = dot(below.astype(bf16), free.astype(bf16))
    here = jnp.where((lane - KEEP).astype(f32) == rank, free, 0.0)
    rest = jnp.sum(here * s.astype(f32), axis=0, keepdims=True)
    row = jnp.where(lane[:1] < KEEP, named.astype(f32), rest)
    room[...] = row.astype(i32)
    return row


def find_way(distances, way):
    sizes = [sum((distances[k] > 1 << bit).astype(i32) for bit in range(TOP)) for k in range(2)]
    way[0] = jnp.where(sizes[1] == TOP, sizes[0], TOP + sizes[1])


def public_kernel(distances, kept, public, acts, coeffs, full, early, pairs, way, room, listed, sems, sem):
    count_x = pairs.shape[0]
    copies = [pltpu.make_async_copy(acts, pairs.at[x, 0], sems.at[x]) for x in range(count_x)]
    for copy in copies:
        copy.start()
    find_way(distances, way)
    row = list_all(kept, room)
    to_scalars = pltpu.make_async_copy(room, listed, sem.at[0])
    to_scalars.start()
    left, right = left_table(spectrum()).astype(bf16), right_table()
    grid = by_halves(lambda x: dot(left, x), dot(public[...], right).astype(bf16))

    def put(s, slab):
        coeffs[s] = slab
        full[s] = slab.astype(bf16)

    to_slabs(grid, put)
    early[LEFT] = jnp.broadcast_to(row, (16, 128)).astype(bf16)
    to_scalars.wait()
    for j in range(LEFT):
        early[j] = full[listed[0, KEEP + j]]
    for copy in copies:
        copy.wait()


def spread_kernel(other, pairs, out, sems):
    copies = [pltpu.make_async_copy(other, out.at[x, 1], sems.at[x]) for x in range(out.shape[0])]
    for copy in copies:
        copy.start()
    for copy in copies:
        copy.wait()


def own_place():
    return lax.axis_index("tp") & 1


def grads_kernel(count, grads, weight, turned, weight_turned):
    place = own_place()
    right = right_table()
    part = grads.shape[0] // 4
    for k in range(4):
        y = dot(grads[k * part : (k + 1) * part], right)
        token = k * part + lines((part, COLS), 0)
        y = jnp.where(token < count[...], y, 0.0).astype(bf16)
        for z in range(2):
            to = k * part + ((z + place) & 1) * (part // 2)
            turned[pl.ds(pl.multiple_of(to, part // 2), part // 2), :] = y[part // 2 * z : part // 2 * (z + 1)]
    weight_turned[...] = dot(weight[...], right).astype(bf16)


def weights_kernel(kept, acts, turned, weight_turned, public_full, packed, full, kept_coeffs, moved, slabs):
    left = split(left_table(spectrum()))
    dims = (((1,), (1,)), ((), ()))
    x = acts[...].reshape(-1, ROWS)
    rows = []
    for h in range(2):
        half = x[:, 128 * h : 128 * (h + 1)]
        row = lax.dot_general(left[0], half, dims, preferred_element_type=f32)
        rows.append((row + lax.dot_general(left[1], half, dims, preferred_element_type=f32)).astype(bf16))
    change = -learn_rate * dot(jnp.concatenate(rows, 0), turned[...])
    moved[...] = change

    def put(s, slab):
        slabs[s] = slab

    to_slabs(by_halves(lambda x: dot(left[0], x), weight_turned[...]) + change, put)
    full[...] = public_full[...]
    for i in range(KEEP):
        s = kept[i]
        slab = slabs[s]
        short = slab.astype(bf16)
        kept_coeffs[i] = slab
        packed[i] = short
        full[s] = short


def fill_kernel(listed, early, peer):
    for j in range(LEFT):
        peer[listed[KEEP + j]] = early[j]
    for i in range(KEEP):
        peer[listed[i]] = jnp.zeros((16, 128), bf16)


def mix(kept, peer, own, kept_coeffs, packed, full, next_coeffs):
    full[...] = own[...]
    for i in range(KEEP):
        s = kept[i]
        value = kept_coeffs[i]
        value = value + step * (peer[s].astype(f32) - value)
        short = value.astype(bf16)
        next_coeffs[i] = value
        packed[i] = short
        full[s] = short


def near_kernel(kept, peer, own, kept_coeffs, packed, full, next_coeffs):
    mix(kept, peer, own, kept_coeffs, packed, full, next_coeffs)


def far_kernel(kept, listed, arrived, filled, own, kept_coeffs, packed, full, next_coeffs, peer):
    peer[...] = filled[...]
    for i in range(KEEP):
        peer[listed[i]] = arrived[i]
    mix(kept, peer, own, kept_coeffs, packed, full, next_coeffs)


def base_kernel(kept, peer, coeffs, kept_coeffs, next_coeffs, moved, weight, out, left_high, right_high, delta):
    delta[...] = step * peer[...].astype(f32) - 2 * step * coeffs[...]
    for i in range(KEEP):
        s = kept[i]
        delta[s] = step * (peer[s].astype(f32) - kept_coeffs[i] - next_coeffs[i])
    grid = from_slabs(lambda s: delta[s]) + moved[...]
    left, right = split(left_table_t()), split(right_table_t())
    left_high[...] = left[0]
    right_high[...] = right[0]
    out[...] = weight[...].astype(f32) + by_halves(lambda x: left_dot(left, x), right_dot(grid, right))


def finish(get, base, left_t, right_t, out):
    grid = (step * from_slabs(lambda s: get(s).astype(f32))).astype(bf16)
    turned = dot(grid, right_t[...]).astype(bf16)
    out[...] = (base[...] + by_halves(lambda x: dot(left_t[...], x), turned)).astype(bf16)


def near_last_kernel(peer, base, left_t, right_t, out):
    finish(lambda s: peer[s], base, left_t, right_t, out)


def far_last_kernel(listed, arrived, filled, base, left_t, right_t, out, slabs):
    slabs[...] = filled[...]
    for i in range(KEEP):
        slabs[listed[i]] = arrived[i]
    finish(lambda s: slabs[s], base, left_t, right_t, out)


def call(kernel, outs, specs, scratch=(), flops=0, moves=0, out_specs=None, aliases=None):
    return pl.pallas_call(
        kernel,
        out_shape=[jax.ShapeDtypeStruct(shape, kind) for shape, kind in outs],
        in_specs=specs,
        out_specs=out_specs or [VM] * len(outs),
        scratch_shapes=list(scratch),
        input_output_aliases=aliases or {},
        compiler_params=pltpu.CompilerParams(vmem_limit_bytes=16 * 2**20),
        cost_estimate=pl.CostEstimate(flops=flops, bytes_accessed=moves, transcendentals=0),
    )


SLAB32 = ((SLABS, 16, 128), f32)
SLAB16 = ((SLABS, 16, 128), bf16)
KEPT32 = ((KEEP, 16, 128), f32)
KEPT16 = ((KEEP, 16, 128), bf16)
GRID32 = ((ROWS, COLS), f32)
GRID16 = ((ROWS, COLS), bf16)
REST = pltpu.SMEM((SLABS + 1,), i32)
ROOM32, ROOM16 = pltpu.VMEM((SLABS, 16, 128), f32), pltpu.VMEM((SLABS, 16, 128), bf16)


ANY = pl.BlockSpec(memory_space=pl.ANY)


def sems(count):
    return pltpu.SemaphoreType.DMA((count,))


def do_public(count, distances, kept, public, acts):
    outs = [SLAB32, SLAB16, ((LEFT + 1, 16, 128), bf16), ((count, 2) + acts.shape, bf16), ((1,), i32)]
    scratch = [pltpu.VMEM((1, 128), i32), pltpu.SMEM((1, 128), i32), sems(count), sems(1)]
    return call(public_kernel, outs, [SM, VM, VM, ANY], scratch, 10**9, 2**21, [VM, VM, VM, ANY, SM])(distances, kept, public, acts)


def do_spread(other, pairs):
    outs = [(pairs.shape, bf16)]
    return call(spread_kernel, outs, [VM, ANY], [sems(pairs.shape[0])], 10**5, 2**20, [ANY], {1: 0})(other, pairs)[0]


def do_grads(count, grads, weight):
    return call(grads_kernel, [(grads.shape, bf16), GRID16], [VM] * 3, (), 2 * 10**9, 2**22)(count, grads, weight)


def do_weights(kept, *rest):
    outs = [KEPT16, SLAB16, KEPT32, GRID32]
    return call(weights_kernel, outs, [SM] + [VM] * 4, [ROOM32], 3 * 10**8, 2**21)(kept, *rest)


def do_fill(listed, early):
    return call(fill_kernel, [SLAB16], [SM, VM], (), 10**6, 2**18)(listed, early)[0]


def do_near(kept, peer, own, kept_coeffs):
    return [*call(near_kernel, [KEPT16, SLAB16, KEPT32], [SM] + [VM] * 3, (), 10**6, 2**19)(kept, peer, own, kept_coeffs), peer]


def do_far(kept, listed, *rest):
    return list(call(far_kernel, [KEPT16, SLAB16, KEPT32, SLAB16], [SM, SM] + [VM] * 4, (), 10**6, 2**19)(kept, listed, *rest))


def do_base(kept, *rest):
    outs = [GRID32, ((128, 128), bf16), ((COLS, COLS), bf16)]
    return call(base_kernel, outs, [SM] + [VM] * 6, [ROOM32], 10**9, 2**22)(kept, *rest)


def do_near_last(*args):
    return call(near_last_kernel, [GRID16], [VM] * 4, (), 2 * 10**8, 2**20)(*args)[0]


def do_far_last(listed, *rest):
    return call(far_last_kernel, [GRID16], [SM] + [VM] * 5, [ROOM16], 2 * 10**8, 2**20)(listed, *rest)[0]


def swapped(block, axis, bit):
    count = lax.axis_size(axis)
    return lax.ppermute(block, axis, [(i, i ^ (1 << bit)) for i in range(count)])


def peers_list(early):
    return early[LEFT, 0, :SLABS].astype(i32)


def shards(activations, out_grads, weight, public, counts, kept, distances):
    count_x = lax.axis_size("tp") // 2
    groups = [[2 * x + z for x in range(count_x)] for z in range(2)]
    acts, grads, weight, public, kept = activations[0], out_grads[0], weight[0], public[0], kept[0, 0]

    other = swapped(acts, "tp", 0)
    coeffs, public_full, early, pairs, way = do_public(count_x, distances, kept[None], public, acts)
    early_far = swapped(early, "rep", TOP)
    pairs = do_spread(other, pairs)
    pairs, counts = lax.optimization_barrier((pairs, counts[:, None]))
    rows = lax.all_to_all(pairs, "tp", 0, 0, axis_index_groups=groups)
    turned, weight_turned = do_grads(counts, grads, weight)
    packed, full, kept_coeffs, moved = do_weights(kept, rows, turned, weight_turned, public_full)

    def rounds(first, second):
        def run(packed, full, early, early_far):
            if first == TOP:
                arrived = swapped(packed, "rep", first)
                if second in PACKED:
                    early, packed = lax.optimization_barrier((early, packed))
                    early_second = swapped(early, "rep", second)
                listed = peers_list(early_far)
                filled = do_fill(listed, early_far)
                packed, full, next_coeffs, peer = do_far(kept, listed, arrived, filled, full, kept_coeffs)
            else:
                early_second = early_far
                packed, full, next_coeffs, peer = do_near(kept, swapped(full, "rep", first), full, kept_coeffs)
            arrived = swapped(packed if second in PACKED else full, "rep", second)
            last = do_base(kept, peer, coeffs, kept_coeffs, next_coeffs, moved, weight)
            if second in PACKED:
                listed = peers_list(early_second)
                return do_far_last(listed, arrived, do_fill(listed, early_second), *last)
            return do_near_last(arrived, *last)

        return run

    ways = [(bit, TOP) for bit in range(TOP)] + [(TOP, bit) for bit in range(TOP)]
    return lax.switch(way[0], [rounds(*pair) for pair in ways], packed, full, early, early_far)[None]


def solution(mesh):
    return jax.shard_map(
        shards,
        mesh=mesh,
        in_specs=(
            P("rep", "tp", None),
            P("rep", None, "tp"),
            P("rep", None, "tp"),
            P("rep", None, "tp"),
            P("rep"),
            P("rep", "tp", None),
            P(),
        ),
        out_specs=P("rep", None, "tp"),
        check_vma=False,
    )
```

```python
import jax
import jax.numpy as jnp
import numpy as np
from jax import lax
from jax.experimental import pallas as pl
from jax.experimental.pallas import tpu as pltpu
from jax.sharding import PartitionSpec as P


learn_rate = 0.02
step = 0.25
ROWS, COLS, KEEP, SLABS, TOP = 256, 512, 40, 64, 5
LEFT = SLABS - KEEP
PACKED = (2, 3, TOP)
f32, bf16, i32 = jnp.float32, jnp.bfloat16, jnp.int32
VM = pl.BlockSpec(memory_space=pltpu.VMEM)
SM = pl.BlockSpec(memory_space=pltpu.SMEM)


def cosines(freq, place):
    phase = ((2 * place + 1) * freq) & 255
    scale = jnp.where(freq == 0, np.float32(np.sqrt(1 / 64)), np.float32(np.sqrt(2 / 64)))
    return scale * jnp.cos(phase.astype(f32) * np.float32(np.pi / 128))


def lines(shape, axis):
    return lax.broadcasted_iota(i32, shape, axis)


def spectrum():
    shape = (64, 128)
    return cosines(lines(shape, 0), lines(shape, 1) & 63)


def left_table(table):
    groups = [table[8 * ub : 8 * ub + 8] for ub in range(8) for _ in range(2)]
    shape = (128, 128)
    return jnp.where((lines(shape, 0) >> 3) & 1 == lines(shape, 1) >> 6, jnp.concatenate(groups, 0), 0.0)


def left_table_t():
    shape = (64, 128)
    r = lines(shape, 1)
    part = cosines((r >> 4) * 8 + (r & 7), lines(shape, 0))
    odd = (r >> 3) & 1
    return jnp.concatenate([jnp.where(odd == 0, part, 0.0), jnp.where(odd == 1, part, 0.0)], 0)


def right_table():
    shape = (64, COLS)
    j = lines(shape, 1)
    part = cosines((j >> 6) * 8 + (j & 7), lines(shape, 0))
    tile = (j >> 3) & 7
    return jnp.concatenate([jnp.where(tile == b, part, 0.0).astype(bf16) for b in range(8)], 0)


def right_table_t():
    table = spectrum()
    low = lines(table.shape, 1) < 64
    masked = jnp.where(low, table, 0.0), jnp.where(low, 0.0, table)
    zeros = jnp.zeros((8, 128), f32)
    columns = []
    for c in range(4):
        groups = [masked[b & 1][8 * vb : 8 * vb + 8] if b >> 1 == c else zeros for vb in range(8) for b in range(8)]
        columns.append(jnp.concatenate(groups, 0))
    return jnp.concatenate(columns, 1)


def dot(a, b):
    return jnp.dot(a, b, preferred_element_type=f32)


def split(x):
    high = x.astype(bf16)
    return high, (x - high.astype(f32)).astype(bf16)


def by_halves(run, x):
    return jnp.concatenate([run(x[:128]), run(x[128:])], 0)


def left_dot(table, x):
    high, low = split(x)
    return dot(table[0], high) + (dot(table[0], low) + dot(table[1], high))


def right_dot(x, table):
    high, low = split(x)
    return dot(high, table[0]) + (dot(low, table[0]) + dot(high, table[1]))


def low_lanes():
    return lax.broadcasted_iota(i32, (128, 128), 1) < 64


def to_slabs(grid, put):
    low = low_lanes()
    for q in range(4):
        top = grid[:128, 128 * q : 128 * (q + 1)]
        bottom = grid[128:, 128 * q : 128 * (q + 1)]
        even = jnp.where(low, top, pltpu.roll(bottom, 64, 1))
        odd = jnp.where(low, pltpu.roll(top, 64, 1), bottom)
        for ub in range(8):
            put(ub * 8 + 2 * q, even[16 * ub : 16 * (ub + 1)])
            put(ub * 8 + 2 * q + 1, odd[16 * ub : 16 * (ub + 1)])


def from_slabs(get):
    low = low_lanes()
    tops, bottoms = [], []
    for q in range(4):
        even = jnp.concatenate([get(ub * 8 + 2 * q) for ub in range(8)], 0)
        odd = jnp.concatenate([get(ub * 8 + 2 * q + 1) for ub in range(8)], 0)
        tops.append(jnp.where(low, even, pltpu.roll(odd, 64, 1)))
        bottoms.append(jnp.where(low, pltpu.roll(even, 64, 1), odd))
    return jnp.concatenate([jnp.concatenate(tops, 1), jnp.concatenate(bottoms, 1)], 0)


def list_all(kept, room):
    room[...] = jnp.full((1, 128), -1, i32)
    room[:, :KEEP] = kept[...]
    named = room[...]
    shape = (SLABS, 128)
    s, lane = lines(shape, 0), lines(shape, 1)
    hits = jnp.where(s == named, 1.0, 0.0)
    free = jnp.broadcast_to(1.0 - jnp.max(hits, axis=1, keepdims=True), shape)
    shape = (SLABS, SLABS)
    below = jnp.where(lines(shape, 1) < lines(shape, 0), 1.0, 0.0)
    rank = dot(below.astype(bf16), free.astype(bf16))
    here = jnp.where((lane - KEEP).astype(f32) == rank, free, 0.0)
    rest = jnp.sum(here * s.astype(f32), axis=0, keepdims=True)
    row = jnp.where(lane[:1] < KEEP, named.astype(f32), rest)
    room[...] = row.astype(i32)
    return row


def find_way(distances, way):
    sizes = [sum((distances[k] > 1 << bit).astype(i32) for bit in range(TOP)) for k in range(2)]
    way[0] = jnp.where(sizes[1] == TOP, sizes[0], TOP + sizes[1])


def public_kernel(distances, kept, public, acts, coeffs, full, early, pairs, way, room, listed, sems, sem):
    count_x = pairs.shape[0]
    copies = [pltpu.make_async_copy(acts, pairs.at[x, 0], sems.at[x]) for x in range(count_x)]
    for copy in copies:
        copy.start()
    find_way(distances, way)
    row = list_all(kept, room)
    to_scalars = pltpu.make_async_copy(room, listed, sem.at[0])
    to_scalars.start()
    left, right = left_table(spectrum()).astype(bf16), right_table()
    grid = by_halves(lambda x: dot(left, x), dot(public[...], right).astype(bf16))

    def put(s, slab):
        coeffs[s] = slab
        full[s] = slab.astype(bf16)

    to_slabs(grid, put)
    early[LEFT] = jnp.broadcast_to(row, (16, 128)).astype(bf16)
    to_scalars.wait()
    for j in range(LEFT):
        early[j] = full[listed[0, KEEP + j]]
    for copy in copies:
        copy.wait()


def spread_kernel(other, pairs, out, sems):
    copies = [pltpu.make_async_copy(other, out.at[x, 1], sems.at[x]) for x in range(out.shape[0])]
    for copy in copies:
        copy.start()
    for copy in copies:
        copy.wait()


def own_place():
    return lax.axis_index("tp") & 1


def grads_kernel(count, grads, weight, turned, weight_coeffs):
    place = own_place()
    right = right_table()
    part = grads.shape[0] // 4
    for k in range(4):
        y = dot(grads[k * part : (k + 1) * part], right)
        token = k * part + lines((part, COLS), 0)
        y = jnp.where(token < count[...], y, 0.0).astype(bf16)
        for z in range(2):
            to = k * part + ((z + place) & 1) * (part // 2)
            turned[pl.ds(pl.multiple_of(to, part // 2), part // 2), :] = y[part // 2 * z : part // 2 * (z + 1)]
    left = left_table(spectrum()).astype(bf16)
    weight_coeffs[...] = by_halves(lambda x: dot(left, x), dot(weight[...], right).astype(bf16))


def weights_kernel(kept_row, acts, turned, weight_coeffs, public_full, packed, full, kept_coeffs, moved, slabs, kept, sem):
    to_scalars = pltpu.make_async_copy(kept_row, kept, sem.at[0])
    to_scalars.start()
    left = split(left_table(spectrum()))
    dims = (((1,), (1,)), ((), ()))
    x = acts[...].reshape(-1, ROWS)
    rows = []
    for h in range(2):
        half = x[:, 128 * h : 128 * (h + 1)]
        row = lax.dot_general(left[0], half, dims, preferred_element_type=f32)
        rows.append((row + lax.dot_general(left[1], half, dims, preferred_element_type=f32)).astype(bf16))
    change = -learn_rate * dot(jnp.concatenate(rows, 0), turned[...])
    moved[...] = change

    def put(s, slab):
        slabs[s] = slab

    to_slabs(weight_coeffs[...] + change, put)
    full[...] = public_full[...]
    to_scalars.wait()
    for i in range(KEEP):
        s = kept[0, i]
        slab = slabs[s]
        short = slab.astype(bf16)
        kept_coeffs[i] = slab
        packed[i] = short
        full[s] = short


def fill_kernel(listed, early, peer):
    for j in range(LEFT):
        peer[listed[KEEP + j]] = early[j]
    for i in range(KEEP):
        peer[listed[i]] = jnp.zeros((16, 128), bf16)


def mix(kept, peer, kept_coeffs, next_coeffs, put):
    for i in range(KEEP):
        s = kept[i]
        value = kept_coeffs[i]
        value = value + step * (peer[s].astype(f32) - value)
        next_coeffs[i] = value
        put(i, s, value.astype(bf16))


def mix_packed(kept, peer, kept_coeffs, packed, next_coeffs):
    def put(i, s, slab):
        packed[i] = slab

    mix(kept, peer, kept_coeffs, next_coeffs, put)


def near_kernel(kept, peer, kept_coeffs, packed, next_coeffs):
    mix_packed(kept, peer, kept_coeffs, packed, next_coeffs)


def unpack(listed, arrived, filled, peer):
    peer[...] = filled[...]
    for i in range(KEEP):
        peer[listed[i]] = arrived[i]


def far_packed_kernel(kept, listed, arrived, filled, kept_coeffs, packed, next_coeffs, peer):
    unpack(listed, arrived, filled, peer)
    mix_packed(kept, peer, kept_coeffs, packed, next_coeffs)


def far_full_kernel(kept, listed, arrived, filled, own, kept_coeffs, full, next_coeffs, peer):
    unpack(listed, arrived, filled, peer)
    full[...] = own[...]

    def put(i, s, slab):
        full[s] = slab

    mix(kept, peer, kept_coeffs, next_coeffs, put)


def base_kernel(kept, peer, coeffs, kept_coeffs, next_coeffs, moved, weight, out, left_high, right_high, delta):
    delta[...] = step * peer[...].astype(f32) - 2 * step * coeffs[...]
    for i in range(KEEP):
        s = kept[i]
        delta[s] = step * (peer[s].astype(f32) - kept_coeffs[i] - next_coeffs[i])
    grid = from_slabs(lambda s: delta[s]) + moved[...]
    left, right = split(left_table_t()), split(right_table_t())
    left_high[...] = left[0]
    right_high[...] = right[0]
    out[...] = weight[...].astype(f32) + by_halves(lambda x: left_dot(left, x), right_dot(grid, right))


def finish(get, base, left_t, right_t, out):
    grid = (step * from_slabs(lambda s: get(s).astype(f32))).astype(bf16)
    turned = dot(grid, right_t[...]).astype(bf16)
    out[...] = (base[...] + by_halves(lambda x: dot(left_t[...], x), turned)).astype(bf16)


def near_last_kernel(peer, base, left_t, right_t, out):
    finish(lambda s: peer[s], base, left_t, right_t, out)


def far_last_kernel(listed, arrived, filled, base, left_t, right_t, out, slabs):
    unpack(listed, arrived, filled, slabs)
    finish(lambda s: slabs[s], base, left_t, right_t, out)


def call(kernel, outs, specs, scratch=(), flops=0, moves=0, out_specs=None, aliases=None):
    return pl.pallas_call(
        kernel,
        out_shape=[jax.ShapeDtypeStruct(shape, kind) for shape, kind in outs],
        in_specs=specs,
        out_specs=out_specs or [VM] * len(outs),
        scratch_shapes=list(scratch),
        input_output_aliases=aliases or {},
        compiler_params=pltpu.CompilerParams(vmem_limit_bytes=16 * 2**20),
        cost_estimate=pl.CostEstimate(flops=flops, bytes_accessed=moves, transcendentals=0),
    )


SLAB32 = ((SLABS, 16, 128), f32)
SLAB16 = ((SLABS, 16, 128), bf16)
KEPT32 = ((KEEP, 16, 128), f32)
KEPT16 = ((KEEP, 16, 128), bf16)
GRID32 = ((ROWS, COLS), f32)
GRID16 = ((ROWS, COLS), bf16)
REST = pltpu.SMEM((SLABS + 1,), i32)
ROOM32, ROOM16 = pltpu.VMEM((SLABS, 16, 128), f32), pltpu.VMEM((SLABS, 16, 128), bf16)


ANY = pl.BlockSpec(memory_space=pl.ANY)


def sems(count):
    return pltpu.SemaphoreType.DMA((count,))


def do_public(count, distances, kept, public, acts):
    outs = [SLAB32, SLAB16, ((LEFT + 1, 16, 128), bf16), ((count, 2) + acts.shape, bf16), ((1,), i32)]
    scratch = [pltpu.VMEM((1, 128), i32), pltpu.SMEM((1, 128), i32), sems(count), sems(1)]
    return call(public_kernel, outs, [SM, VM, VM, ANY], scratch, 10**9, 2**21, [VM, VM, VM, ANY, SM])(distances, kept, public, acts)


def do_spread(other, pairs):
    outs = [(pairs.shape, bf16)]
    return call(spread_kernel, outs, [VM, ANY], [sems(pairs.shape[0])], 10**5, 2**20, [ANY], {1: 0})(other, pairs)[0]


def do_grads(count, grads, weight):
    return call(grads_kernel, [(grads.shape, bf16), GRID32], [VM] * 3, (), 2 * 10**9, 2**22)(count, grads, weight)


def do_weights(kept, *rest):
    outs = [KEPT16, SLAB16, KEPT32, GRID32]
    return call(weights_kernel, outs, [VM] * 5, [ROOM32, pltpu.SMEM((1, KEEP), i32), sems(1)], 3 * 10**8, 2**21)(kept, *rest)


def do_fill(listed, early):
    return call(fill_kernel, [SLAB16], [SM, VM], (), 10**6, 2**18)(listed, early)[0]


def do_near(kept, peer, kept_coeffs):
    return call(near_kernel, [KEPT16, KEPT32], [SM] + [VM] * 2, (), 10**6, 2**19)(kept, peer, kept_coeffs)


def do_far_packed(kept, listed, *rest):
    return call(far_packed_kernel, [KEPT16, KEPT32, SLAB16], [SM, SM] + [VM] * 3, (), 10**6, 2**19)(kept, listed, *rest)


def do_far_full(kept, listed, *rest):
    return call(far_full_kernel, [SLAB16, KEPT32, SLAB16], [SM, SM] + [VM] * 4, (), 10**6, 2**19)(kept, listed, *rest)


def do_base(kept, *rest):
    outs = [GRID32, ((128, 128), bf16), ((COLS, COLS), bf16)]
    return call(base_kernel, outs, [SM] + [VM] * 6, [ROOM32], 10**9, 2**22)(kept, *rest)


def do_near_last(*args):
    return call(near_last_kernel, [GRID16], [VM] * 4, (), 2 * 10**8, 2**20)(*args)[0]


def do_far_last(listed, *rest):
    return call(far_last_kernel, [GRID16], [SM] + [VM] * 5, [ROOM16], 2 * 10**8, 2**20)(listed, *rest)[0]


def swapped(block, axis, bit):
    count = lax.axis_size(axis)
    return lax.ppermute(block, axis, [(i, i ^ (1 << bit)) for i in range(count)])


def peers_list(early):
    return early[LEFT, 0, :SLABS].astype(i32)


def shards(activations, out_grads, weight, public, counts, kept, distances):
    count_x = lax.axis_size("tp") // 2
    groups = [[2 * x + z for x in range(count_x)] for z in range(2)]
    acts, grads, weight, public, kept = activations[0], out_grads[0], weight[0], public[0], kept[0, 0]

    other = swapped(acts, "tp", 0)
    coeffs, public_full, early, pairs, way = do_public(count_x, distances, kept[None], public, acts)
    early_far = swapped(early, "rep", TOP)
    pairs = do_spread(other, pairs)
    pairs, counts = lax.optimization_barrier((pairs, counts[:, None]))
    rows = lax.all_to_all(pairs, "tp", 0, 0, axis_index_groups=groups)
    turned, weight_coeffs = do_grads(counts, grads, weight)
    packed, full, kept_coeffs, moved = do_weights(kept[None], rows, turned, weight_coeffs, public_full)

    def rounds(first, second):
        def run(packed, full, early, early_far):
            if first == TOP:
                arrived = swapped(packed, "rep", first)
                if second in PACKED:
                    early, packed = lax.optimization_barrier((early, packed))
                    early_second = swapped(early, "rep", second)
                listed = peers_list(early_far)
                filled = do_fill(listed, early_far)
                if second in PACKED:
                    late, next_coeffs, peer = do_far_packed(kept, listed, arrived, filled, kept_coeffs)
                else:
                    late, next_coeffs, peer = do_far_full(kept, listed, arrived, filled, full, kept_coeffs)
            else:
                early_second = early_far
                peer = swapped(full, "rep", first)
                late, next_coeffs = do_near(kept, peer, kept_coeffs)
            arrived = swapped(late, "rep", second)
            last = do_base(kept, peer, coeffs, kept_coeffs, next_coeffs, moved, weight)
            if second in PACKED:
                listed = peers_list(early_second)
                return do_far_last(listed, arrived, do_fill(listed, early_second), *last)
            return do_near_last(arrived, *last)

        return run

    ways = [(bit, TOP) for bit in range(TOP)] + [(TOP, bit) for bit in range(TOP)]
    return lax.switch(way[0], [rounds(*pair) for pair in ways], packed, full, early, early_far)[None]


def solution(mesh):
    return jax.shard_map(
        shards,
        mesh=mesh,
        in_specs=(
            P("rep", "tp", None),
            P("rep", None, "tp"),
            P("rep", None, "tp"),
            P("rep", None, "tp"),
            P("rep"),
            P("rep", "tp", None),
            P(),
        ),
        out_specs=P("rep", None, "tp"),
        check_vma=False,
    )
```

```python
import jax
import jax.numpy as jnp
import numpy as np
from jax import lax
from jax.experimental import pallas as pl
from jax.experimental.pallas import tpu as pltpu
from jax.sharding import PartitionSpec as P


learn_rate = 0.02
step = 0.25
ROWS, COLS, KEEP, SLABS, TOP = 256, 512, 40, 64, 5
LEFT = SLABS - KEEP
PACKED = (2, 3, TOP)
f32, bf16, i32 = jnp.float32, jnp.bfloat16, jnp.int32
VM = pl.BlockSpec(memory_space=pltpu.VMEM)
SM = pl.BlockSpec(memory_space=pltpu.SMEM)


def cosines(freq, place):
    phase = ((2 * place + 1) * freq) & 255
    scale = jnp.where(freq == 0, np.float32(np.sqrt(1 / 64)), np.float32(np.sqrt(2 / 64)))
    return scale * jnp.cos(phase.astype(f32) * np.float32(np.pi / 128))


def lines(shape, axis):
    return lax.broadcasted_iota(i32, shape, axis)


def spectrum():
    shape = (64, 128)
    return cosines(lines(shape, 0), lines(shape, 1) & 63)


def left_table(table):
    groups = [table[8 * ub : 8 * ub + 8] for ub in range(8) for _ in range(2)]
    shape = (128, 128)
    return jnp.where((lines(shape, 0) >> 3) & 1 == lines(shape, 1) >> 6, jnp.concatenate(groups, 0), 0.0)


def left_table_t():
    shape = (64, 128)
    r = lines(shape, 1)
    part = cosines((r >> 4) * 8 + (r & 7), lines(shape, 0))
    odd = (r >> 3) & 1
    return jnp.concatenate([jnp.where(odd == 0, part, 0.0), jnp.where(odd == 1, part, 0.0)], 0)


def right_table():
    shape = (64, COLS)
    j = lines(shape, 1)
    part = cosines((j >> 6) * 8 + (j & 7), lines(shape, 0))
    tile = (j >> 3) & 7
    return jnp.concatenate([jnp.where(tile == b, part, 0.0).astype(bf16) for b in range(8)], 0)


def right_table_t():
    table = spectrum()
    low = lines(table.shape, 1) < 64
    masked = jnp.where(low, table, 0.0), jnp.where(low, 0.0, table)
    zeros = jnp.zeros((8, 128), f32)
    columns = []
    for c in range(4):
        groups = [masked[b & 1][8 * vb : 8 * vb + 8] if b >> 1 == c else zeros for vb in range(8) for b in range(8)]
        columns.append(jnp.concatenate(groups, 0))
    return jnp.concatenate(columns, 1)


def dot(a, b):
    return jnp.dot(a, b, preferred_element_type=f32)


def split(x):
    high = x.astype(bf16)
    return high, (x - high.astype(f32)).astype(bf16)


def by_halves(run, x):
    return jnp.concatenate([run(x[:128]), run(x[128:])], 0)


def left_dot(table, x):
    high, low = split(x)
    return dot(table[0], high) + (dot(table[0], low) + dot(table[1], high))


def right_dot(x, table):
    high, low = split(x)
    return dot(high, table[0]) + (dot(low, table[0]) + dot(high, table[1]))


def low_lanes():
    return lax.broadcasted_iota(i32, (128, 128), 1) < 64


def to_slabs(grid, put):
    low = low_lanes()
    for q in range(4):
        top = grid[:128, 128 * q : 128 * (q + 1)]
        bottom = grid[128:, 128 * q : 128 * (q + 1)]
        even = jnp.where(low, top, pltpu.roll(bottom, 64, 1))
        odd = jnp.where(low, pltpu.roll(top, 64, 1), bottom)
        for ub in range(8):
            put(ub * 8 + 2 * q, even[16 * ub : 16 * (ub + 1)])
            put(ub * 8 + 2 * q + 1, odd[16 * ub : 16 * (ub + 1)])


def from_slabs(get):
    low = low_lanes()
    tops, bottoms = [], []
    for q in range(4):
        even = jnp.concatenate([get(ub * 8 + 2 * q) for ub in range(8)], 0)
        odd = jnp.concatenate([get(ub * 8 + 2 * q + 1) for ub in range(8)], 0)
        tops.append(jnp.where(low, even, pltpu.roll(odd, 64, 1)))
        bottoms.append(jnp.where(low, pltpu.roll(even, 64, 1), odd))
    return jnp.concatenate([jnp.concatenate(tops, 1), jnp.concatenate(bottoms, 1)], 0)


def list_all(kept, room):
    room[...] = jnp.full((1, 128), -1, i32)
    room[:, :KEEP] = kept[...]
    named = room[...]
    shape = (SLABS, 128)
    s, lane = lines(shape, 0), lines(shape, 1)
    hits = jnp.where(s == named, 1.0, 0.0)
    free = jnp.broadcast_to(1.0 - jnp.max(hits, axis=1, keepdims=True), shape)
    shape = (SLABS, SLABS)
    below = jnp.where(lines(shape, 1) < lines(shape, 0), 1.0, 0.0)
    rank = dot(below.astype(bf16), free.astype(bf16))
    here = jnp.where((lane - KEEP).astype(f32) == rank, free, 0.0)
    rest = jnp.sum(here * s.astype(f32), axis=0, keepdims=True)
    row = jnp.where(lane[:1] < KEEP, named.astype(f32), rest)
    room[...] = row.astype(i32)
    return row


def find_way(distances, way):
    sizes = [sum((distances[k] > 1 << bit).astype(i32) for bit in range(TOP)) for k in range(2)]
    way[0] = jnp.where(sizes[1] == TOP, sizes[0], TOP + sizes[1])


def public_kernel(distances, kept, public, full, early, way, room, listed, sem):
    find_way(distances, way)
    row = list_all(kept, room)
    to_scalars = pltpu.make_async_copy(room, listed, sem.at[0])
    to_scalars.start()
    left, right = left_table(spectrum()).astype(bf16), right_table()
    grid = by_halves(lambda x: dot(left, x), dot(public[...], right).astype(bf16))

    def put(s, slab):
        full[s] = slab.astype(bf16)

    to_slabs(grid, put)
    early[LEFT] = jnp.broadcast_to(row, (16, 128)).astype(bf16)
    to_scalars.wait()
    for j in range(LEFT):
        early[j] = full[listed[0, KEEP + j]]


def spread_kernel(own, other, out, sems):
    copies = []
    for x in range(out.shape[0]):
        for k, part in enumerate((own, other)):
            copies.append(pltpu.make_async_copy(part, out.at[x, k], sems.at[2 * x + k]))
    for copy in copies:
        copy.start()
    for copy in copies:
        copy.wait()


def own_place():
    return lax.axis_index("tp") & 1


def grads_kernel(count, grads, weight, turned, weight_coeffs):
    place = own_place()
    right = right_table()
    part = grads.shape[0] // 4
    for k in range(4):
        y = dot(grads[k * part : (k + 1) * part], right)
        token = k * part + lines((part, COLS), 0)
        y = jnp.where(token < count[...], y, 0.0).astype(bf16)
        for z in range(2):
            to = k * part + ((z + place) & 1) * (part // 2)
            turned[pl.ds(pl.multiple_of(to, part // 2), part // 2), :] = y[part // 2 * z : part // 2 * (z + 1)]
    left = left_table(spectrum()).astype(bf16)
    weight_coeffs[...] = by_halves(lambda x: dot(left, x), dot(weight[...], right).astype(bf16))


def weights_kernel(kept_row, acts, turned, weight_coeffs, public_full, packed, full, kept_coeffs, moved, slabs, kept, sem):
    to_scalars = pltpu.make_async_copy(kept_row, kept, sem.at[0])
    to_scalars.start()
    left = split(left_table(spectrum()))
    dims = (((1,), (1,)), ((), ()))
    x = acts[...].reshape(-1, ROWS)
    rows = []
    for h in range(2):
        half = x[:, 128 * h : 128 * (h + 1)]
        row = lax.dot_general(left[0], half, dims, preferred_element_type=f32)
        rows.append((row + lax.dot_general(left[1], half, dims, preferred_element_type=f32)).astype(bf16))
    change = -learn_rate * dot(jnp.concatenate(rows, 0), turned[...])
    moved[...] = change

    def put(s, slab):
        slabs[s] = slab

    to_slabs(weight_coeffs[...] + change, put)
    full[...] = public_full[...]
    to_scalars.wait()
    for i in range(KEEP):
        s = kept[0, i]
        slab = slabs[s]
        short = slab.astype(bf16)
        kept_coeffs[i] = slab
        packed[i] = short
        full[s] = short


def fill_kernel(listed, early, peer):
    for j in range(LEFT):
        peer[listed[KEEP + j]] = early[j]
    for i in range(KEEP):
        peer[listed[i]] = jnp.zeros((16, 128), bf16)


def mix(kept, peer, kept_coeffs, next_coeffs, put):
    for i in range(KEEP):
        s = kept[i]
        value = kept_coeffs[i]
        value = value + step * (peer[s].astype(f32) - value)
        next_coeffs[i] = value
        put(i, s, value.astype(bf16))


def mix_packed(kept, peer, kept_coeffs, packed, next_coeffs):
    def put(i, s, slab):
        packed[i] = slab

    mix(kept, peer, kept_coeffs, next_coeffs, put)


def near_kernel(kept, peer, kept_coeffs, packed, next_coeffs):
    mix_packed(kept, peer, kept_coeffs, packed, next_coeffs)


def unpack(listed, arrived, filled, peer):
    peer[...] = filled[...]
    for i in range(KEEP):
        peer[listed[i]] = arrived[i]


def far_packed_kernel(kept, listed, arrived, filled, kept_coeffs, packed, next_coeffs, peer):
    unpack(listed, arrived, filled, peer)
    mix_packed(kept, peer, kept_coeffs, packed, next_coeffs)


def far_full_kernel(kept, listed, arrived, filled, own, kept_coeffs, full, next_coeffs, peer):
    unpack(listed, arrived, filled, peer)
    full[...] = own[...]

    def put(i, s, slab):
        full[s] = slab

    mix(kept, peer, kept_coeffs, next_coeffs, put)


def base_kernel(kept, peer, public_full, kept_coeffs, next_coeffs, moved, weight, out, left_high, right_high, delta):
    delta[...] = step * peer[...].astype(f32) - 2 * step * public_full[...].astype(f32)
    for i in range(KEEP):
        s = kept[i]
        delta[s] = step * (peer[s].astype(f32) - kept_coeffs[i] - next_coeffs[i])
    grid = from_slabs(lambda s: delta[s]) + moved[...]
    left, right = split(left_table_t()), split(right_table_t())
    left_high[...] = left[0]
    right_high[...] = right[0]
    out[...] = weight[...].astype(f32) + by_halves(lambda x: left_dot(left, x), right_dot(grid, right))


def finish(get, base, left_t, right_t, out):
    grid = (step * from_slabs(lambda s: get(s).astype(f32))).astype(bf16)
    turned = dot(grid, right_t[...]).astype(bf16)
    out[...] = (base[...] + by_halves(lambda x: dot(left_t[...], x), turned)).astype(bf16)


def near_last_kernel(peer, base, left_t, right_t, out):
    finish(lambda s: peer[s], base, left_t, right_t, out)


def far_last_kernel(listed, arrived, filled, base, left_t, right_t, out, slabs):
    unpack(listed, arrived, filled, slabs)
    finish(lambda s: slabs[s], base, left_t, right_t, out)


def call(kernel, outs, specs, scratch=(), flops=0, moves=0, out_specs=None):
    return pl.pallas_call(
        kernel,
        out_shape=[jax.ShapeDtypeStruct(shape, kind) for shape, kind in outs],
        in_specs=specs,
        out_specs=out_specs or [VM] * len(outs),
        scratch_shapes=list(scratch),
        compiler_params=pltpu.CompilerParams(vmem_limit_bytes=16 * 2**20),
        cost_estimate=pl.CostEstimate(flops=flops, bytes_accessed=moves, transcendentals=0),
    )


SLAB16 = ((SLABS, 16, 128), bf16)
KEPT32 = ((KEEP, 16, 128), f32)
KEPT16 = ((KEEP, 16, 128), bf16)
GRID32 = ((ROWS, COLS), f32)
GRID16 = ((ROWS, COLS), bf16)
REST = pltpu.SMEM((SLABS + 1,), i32)
ROOM32, ROOM16 = pltpu.VMEM((SLABS, 16, 128), f32), pltpu.VMEM((SLABS, 16, 128), bf16)


ANY = pl.BlockSpec(memory_space=pl.ANY)


def sems(count):
    return pltpu.SemaphoreType.DMA((count,))


def do_public(distances, kept, public):
    outs = [SLAB16, ((LEFT + 1, 16, 128), bf16), ((1,), i32)]
    scratch = [pltpu.VMEM((1, 128), i32), pltpu.SMEM((1, 128), i32), sems(1)]
    return call(public_kernel, outs, [SM, VM, VM], scratch, 10**9, 2**21, [VM, VM, SM])(distances, kept, public)


def do_spread(count, own, other):
    outs = [((count, 2) + own.shape, bf16)]
    return call(spread_kernel, outs, [VM, VM], [sems(2 * count)], 10**5, 2**20, [ANY])(own, other)[0]


def do_grads(count, grads, weight):
    return call(grads_kernel, [(grads.shape, bf16), GRID32], [VM] * 3, (), 2 * 10**9, 2**22)(count, grads, weight)


def do_weights(kept, *rest):
    outs = [KEPT16, SLAB16, KEPT32, GRID32]
    return call(weights_kernel, outs, [VM] * 5, [ROOM32, pltpu.SMEM((1, KEEP), i32), sems(1)], 3 * 10**8, 2**21)(kept, *rest)


def do_fill(listed, early):
    return call(fill_kernel, [SLAB16], [SM, VM], (), 10**6, 2**18)(listed, early)[0]


def do_near(kept, peer, kept_coeffs):
    return call(near_kernel, [KEPT16, KEPT32], [SM] + [VM] * 2, (), 10**6, 2**19)(kept, peer, kept_coeffs)


def do_far_packed(kept, listed, *rest):
    return call(far_packed_kernel, [KEPT16, KEPT32, SLAB16], [SM, SM] + [VM] * 3, (), 10**6, 2**19)(kept, listed, *rest)


def do_far_full(kept, listed, *rest):
    return call(far_full_kernel, [SLAB16, KEPT32, SLAB16], [SM, SM] + [VM] * 4, (), 10**6, 2**19)(kept, listed, *rest)


def do_base(kept, *rest):
    outs = [GRID32, ((128, 128), bf16), ((COLS, COLS), bf16)]
    return call(base_kernel, outs, [SM] + [VM] * 6, [ROOM32], 10**9, 2**22)(kept, *rest)


def do_near_last(*args):
    return call(near_last_kernel, [GRID16], [VM] * 4, (), 2 * 10**8, 2**20)(*args)[0]


def do_far_last(listed, *rest):
    return call(far_last_kernel, [GRID16], [SM] + [VM] * 5, [ROOM16], 2 * 10**8, 2**20)(listed, *rest)[0]


def swapped(block, axis, bit):
    count = lax.axis_size(axis)
    return lax.ppermute(block, axis, [(i, i ^ (1 << bit)) for i in range(count)])


def peers_list(early):
    return early[LEFT, 0, :SLABS].astype(i32)


def shards(activations, out_grads, weight, public, counts, kept, distances):
    count_x = lax.axis_size("tp") // 2
    groups = [[2 * x + z for x in range(count_x)] for z in range(2)]
    acts, grads, weight, public, kept = activations[0], out_grads[0], weight[0], public[0], kept[0, 0]

    other = swapped(acts, "tp", 0)
    public_full, early, way = do_public(distances, kept[None], public)
    early_far = swapped(early, "rep", TOP)
    other, early = lax.optimization_barrier((other, early))
    pairs = do_spread(count_x, acts, other)
    pairs, counts = lax.optimization_barrier((pairs, counts[:, None]))
    rows = lax.all_to_all(pairs, "tp", 0, 0, axis_index_groups=groups)
    turned, weight_coeffs = do_grads(counts, grads, weight)
    packed, full, kept_coeffs, moved = do_weights(kept[None], rows, turned, weight_coeffs, public_full)

    def rounds(first, second):
        def run(packed, full, early, early_far):
            if first == TOP:
                arrived = swapped(packed, "rep", first)
                if second in PACKED:
                    early, packed = lax.optimization_barrier((early, packed))
                    early_second = swapped(early, "rep", second)
                listed = peers_list(early_far)
                filled = do_fill(listed, early_far)
                if second in PACKED:
                    late, next_coeffs, peer = do_far_packed(kept, listed, arrived, filled, kept_coeffs)
                else:
                    late, next_coeffs, peer = do_far_full(kept, listed, arrived, filled, full, kept_coeffs)
            else:
                early_second = early_far
                peer = swapped(full, "rep", first)
                late, next_coeffs = do_near(kept, peer, kept_coeffs)
            arrived = swapped(late, "rep", second)
            last = do_base(kept, peer, public_full, kept_coeffs, next_coeffs, moved, weight)
            if second in PACKED:
                listed = peers_list(early_second)
                return do_far_last(listed, arrived, do_fill(listed, early_second), *last)
            return do_near_last(arrived, *last)

        return run

    ways = [(bit, TOP) for bit in range(TOP)] + [(TOP, bit) for bit in range(TOP)]
    return lax.switch(way[0], [rounds(*pair) for pair in ways], packed, full, early, early_far)[None]


def solution(mesh):
    return jax.shard_map(
        shards,
        mesh=mesh,
        in_specs=(
            P("rep", "tp", None),
            P("rep", None, "tp"),
            P("rep", None, "tp"),
            P("rep", None, "tp"),
            P("rep"),
            P("rep", "tp", None),
            P(),
        ),
        out_specs=P("rep", None, "tp"),
        check_vma=False,
    )
```

```python
import jax
import jax.numpy as jnp
import numpy as np
from jax import lax
from jax.experimental import pallas as pl
from jax.experimental.pallas import tpu as pltpu
from jax.sharding import PartitionSpec as P


learn_rate = 0.02
step = 0.25
ROWS, COLS, KEEP, SLABS, TOP = 256, 512, 40, 64, 5
LEFT = SLABS - KEEP
PACKED = (1, 2, 3, 4, TOP)
f32, bf16, i32 = jnp.float32, jnp.bfloat16, jnp.int32
VM = pl.BlockSpec(memory_space=pltpu.VMEM)
SM = pl.BlockSpec(memory_space=pltpu.SMEM)


def cosines(freq, place):
    phase = ((2 * place + 1) * freq) & 255
    scale = jnp.where(freq == 0, np.float32(np.sqrt(1 / 64)), np.float32(np.sqrt(2 / 64)))
    return scale * jnp.cos(phase.astype(f32) * np.float32(np.pi / 128))


def lines(shape, axis):
    return lax.broadcasted_iota(i32, shape, axis)


def spectrum():
    shape = (64, 128)
    return cosines(lines(shape, 0), lines(shape, 1) & 63)


def left_table(table):
    groups = [table[8 * ub : 8 * ub + 8] for ub in range(8) for _ in range(2)]
    shape = (128, 128)
    return jnp.where((lines(shape, 0) >> 3) & 1 == lines(shape, 1) >> 6, jnp.concatenate(groups, 0), 0.0)


def left_table_t():
    shape = (64, 128)
    r = lines(shape, 1)
    part = cosines((r >> 4) * 8 + (r & 7), lines(shape, 0))
    odd = (r >> 3) & 1
    return jnp.concatenate([jnp.where(odd == 0, part, 0.0), jnp.where(odd == 1, part, 0.0)], 0)


def right_table():
    shape = (64, COLS)
    j = lines(shape, 1)
    part = cosines((j >> 6) * 8 + (j & 7), lines(shape, 0))
    tile = (j >> 3) & 7
    return jnp.concatenate([jnp.where(tile == b, part, 0.0).astype(bf16) for b in range(8)], 0)


def right_table_t():
    table = spectrum()
    low = lines(table.shape, 1) < 64
    masked = jnp.where(low, table, 0.0), jnp.where(low, 0.0, table)
    zeros = jnp.zeros((8, 128), f32)
    columns = []
    for c in range(4):
        groups = [masked[b & 1][8 * vb : 8 * vb + 8] if b >> 1 == c else zeros for vb in range(8) for b in range(8)]
        columns.append(jnp.concatenate(groups, 0))
    return jnp.concatenate(columns, 1)


def dot(a, b):
    return jnp.dot(a, b, preferred_element_type=f32)


def split(x):
    high = x.astype(bf16)
    return high, (x - high.astype(f32)).astype(bf16)


def by_halves(run, x):
    return jnp.concatenate([run(x[:128]), run(x[128:])], 0)


def left_dot(table, x):
    high, low = split(x)
    return dot(table[0], high) + (dot(table[0], low) + dot(table[1], high))


def right_dot(x, table):
    high, low = split(x)
    return dot(high, table[0]) + (dot(low, table[0]) + dot(high, table[1]))


def low_lanes():
    return lax.broadcasted_iota(i32, (128, 128), 1) < 64


def to_slabs(grid, put):
    low = low_lanes()
    for q in range(4):
        top = grid[:128, 128 * q : 128 * (q + 1)]
        bottom = grid[128:, 128 * q : 128 * (q + 1)]
        even = jnp.where(low, top, pltpu.roll(bottom, 64, 1))
        odd = jnp.where(low, pltpu.roll(top, 64, 1), bottom)
        for ub in range(8):
            put(ub * 8 + 2 * q, even[16 * ub : 16 * (ub + 1)])
            put(ub * 8 + 2 * q + 1, odd[16 * ub : 16 * (ub + 1)])


def from_slabs(get):
    low = low_lanes()
    tops, bottoms = [], []
    for q in range(4):
        even = jnp.concatenate([get(ub * 8 + 2 * q) for ub in range(8)], 0)
        odd = jnp.concatenate([get(ub * 8 + 2 * q + 1) for ub in range(8)], 0)
        tops.append(jnp.where(low, even, pltpu.roll(odd, 64, 1)))
        bottoms.append(jnp.where(low, pltpu.roll(even, 64, 1), odd))
    return jnp.concatenate([jnp.concatenate(tops, 1), jnp.concatenate(bottoms, 1)], 0)


def list_all(kept, room):
    room[...] = jnp.full((1, 128), -1, i32)
    room[:, :KEEP] = kept[...]
    named = room[...]
    shape = (SLABS, 128)
    s, lane = lines(shape, 0), lines(shape, 1)
    hits = jnp.where(s == named, 1.0, 0.0)
    free = jnp.broadcast_to(1.0 - jnp.max(hits, axis=1, keepdims=True), shape)
    shape = (SLABS, SLABS)
    below = jnp.where(lines(shape, 1) < lines(shape, 0), 1.0, 0.0)
    rank = dot(below.astype(bf16), free.astype(bf16))
    here = jnp.where((lane - KEEP).astype(f32) == rank, free, 0.0)
    rest = jnp.sum(here * s.astype(f32), axis=0, keepdims=True)
    row = jnp.where(lane[:1] < KEEP, named.astype(f32), rest)
    room[...] = row.astype(i32)
    return row


def find_way(distances, way):
    sizes = [sum((distances[k] > 1 << bit).astype(i32) for bit in range(TOP)) for k in range(2)]
    way[0] = jnp.where(sizes[1] == TOP, sizes[0], TOP + sizes[1])


def public_kernel(distances, kept, public, full, early, way, room, listed, sem):
    find_way(distances, way)
    row = list_all(kept, room)
    to_scalars = pltpu.make_async_copy(room, listed, sem.at[0])
    to_scalars.start()
    left, right = left_table(spectrum()).astype(bf16), right_table()
    grid = by_halves(lambda x: dot(left, x), dot(public[...], right).astype(bf16))

    def put(s, slab):
        full[s] = slab.astype(bf16)

    to_slabs(grid, put)
    early[LEFT] = jnp.broadcast_to(row, (16, 128)).astype(bf16)
    to_scalars.wait()
    for j in range(LEFT):
        early[j] = full[listed[0, KEEP + j]]


def spread_kernel(own, other, out, sems):
    copies = []
    for x in range(out.shape[0]):
        for k, part in enumerate((own, other)):
            copies.append(pltpu.make_async_copy(part, out.at[x, k], sems.at[2 * x + k]))
    for copy in copies:
        copy.start()
    for copy in copies:
        copy.wait()


def own_place():
    return lax.axis_index("tp") & 1


def grads_kernel(count, grads, weight, turned, weight_coeffs):
    place = own_place()
    right = right_table()
    part = grads.shape[0] // 4
    for k in range(4):
        y = dot(grads[k * part : (k + 1) * part], right)
        token = k * part + lines((part, COLS), 0)
        y = jnp.where(token < count[...], y, 0.0).astype(bf16)
        for z in range(2):
            to = k * part + ((z + place) & 1) * (part // 2)
            turned[pl.ds(pl.multiple_of(to, part // 2), part // 2), :] = y[part // 2 * z : part // 2 * (z + 1)]
    left = left_table(spectrum()).astype(bf16)
    weight_coeffs[...] = by_halves(lambda x: dot(left, x), dot(weight[...], right).astype(bf16))


def weights_kernel(kept_row, acts, turned, weight_coeffs, public_full, packed, full, kept_coeffs, moved, slabs, kept, sem):
    to_scalars = pltpu.make_async_copy(kept_row, kept, sem.at[0])
    to_scalars.start()
    left = split(left_table(spectrum()))
    dims = (((1,), (1,)), ((), ()))
    x = acts[...].reshape(-1, ROWS)
    rows = []
    for h in range(2):
        half = x[:, 128 * h : 128 * (h + 1)]
        row = lax.dot_general(left[0], half, dims, preferred_element_type=f32)
        rows.append((row + lax.dot_general(left[1], half, dims, preferred_element_type=f32)).astype(bf16))
    change = -learn_rate * dot(jnp.concatenate(rows, 0), turned[...])
    moved[...] = change

    def put(s, slab):
        slabs[s] = slab

    to_slabs(weight_coeffs[...] + change, put)
    full[...] = public_full[...]
    to_scalars.wait()
    for i in range(KEEP):
        s = kept[0, i]
        slab = slabs[s]
        short = slab.astype(bf16)
        kept_coeffs[i] = slab
        packed[i] = short
        full[s] = short


def fill_kernel(listed, early, peer):
    for j in range(LEFT):
        peer[listed[KEEP + j]] = early[j]
    for i in range(KEEP):
        peer[listed[i]] = jnp.zeros((16, 128), bf16)


def mix(kept, peer, kept_coeffs, next_coeffs, put):
    for i in range(KEEP):
        s = kept[i]
        value = kept_coeffs[i]
        value = value + step * (peer[s].astype(f32) - value)
        next_coeffs[i] = value
        put(i, s, value.astype(bf16))


def mix_packed(kept, peer, kept_coeffs, packed, next_coeffs):
    def put(i, s, slab):
        packed[i] = slab

    mix(kept, peer, kept_coeffs, next_coeffs, put)


def near_kernel(kept, peer, kept_coeffs, packed, next_coeffs):
    mix_packed(kept, peer, kept_coeffs, packed, next_coeffs)


def unpack(listed, arrived, filled, peer):
    peer[...] = filled[...]
    for i in range(KEEP):
        peer[listed[i]] = arrived[i]


def far_packed_kernel(kept, listed, arrived, filled, kept_coeffs, packed, next_coeffs, peer):
    unpack(listed, arrived, filled, peer)
    mix_packed(kept, peer, kept_coeffs, packed, next_coeffs)


def far_full_kernel(kept, listed, arrived, filled, own, kept_coeffs, full, next_coeffs, peer):
    unpack(listed, arrived, filled, peer)
    full[...] = own[...]

    def put(i, s, slab):
        full[s] = slab

    mix(kept, peer, kept_coeffs, next_coeffs, put)


def base_kernel(kept, peer, public_full, kept_coeffs, next_coeffs, moved, weight, out, left_high, right_high, delta):
    delta[...] = step * peer[...].astype(f32) - 2 * step * public_full[...].astype(f32)
    for i in range(KEEP):
        s = kept[i]
        delta[s] = step * (peer[s].astype(f32) - kept_coeffs[i] - next_coeffs[i])
    grid = from_slabs(lambda s: delta[s]) + moved[...]
    left, right = split(left_table_t()), split(right_table_t())
    left_high[...] = left[0]
    right_high[...] = right[0]
    out[...] = weight[...].astype(f32) + by_halves(lambda x: left_dot(left, x), right_dot(grid, right))


def finish(get, base, left_t, right_t, out):
    grid = (step * from_slabs(lambda s: get(s).astype(f32))).astype(bf16)
    turned = dot(grid, right_t[...]).astype(bf16)
    out[...] = (base[...] + by_halves(lambda x: dot(left_t[...], x), turned)).astype(bf16)


def near_last_kernel(peer, base, left_t, right_t, out):
    finish(lambda s: peer[s], base, left_t, right_t, out)


def far_last_kernel(listed, arrived, filled, base, left_t, right_t, out, slabs):
    unpack(listed, arrived, filled, slabs)
    finish(lambda s: slabs[s], base, left_t, right_t, out)


def call(kernel, outs, specs, scratch=(), flops=0, moves=0, out_specs=None):
    return pl.pallas_call(
        kernel,
        out_shape=[jax.ShapeDtypeStruct(shape, kind) for shape, kind in outs],
        in_specs=specs,
        out_specs=out_specs or [VM] * len(outs),
        scratch_shapes=list(scratch),
        compiler_params=pltpu.CompilerParams(vmem_limit_bytes=16 * 2**20),
        cost_estimate=pl.CostEstimate(flops=flops, bytes_accessed=moves, transcendentals=0),
    )


SLAB16 = ((SLABS, 16, 128), bf16)
KEPT32 = ((KEEP, 16, 128), f32)
KEPT16 = ((KEEP, 16, 128), bf16)
GRID32 = ((ROWS, COLS), f32)
GRID16 = ((ROWS, COLS), bf16)
REST = pltpu.SMEM((SLABS + 1,), i32)
ROOM32, ROOM16 = pltpu.VMEM((SLABS, 16, 128), f32), pltpu.VMEM((SLABS, 16, 128), bf16)


ANY = pl.BlockSpec(memory_space=pl.ANY)


def sems(count):
    return pltpu.SemaphoreType.DMA((count,))


def do_public(distances, kept, public):
    outs = [SLAB16, ((LEFT + 1, 16, 128), bf16), ((1,), i32)]
    scratch = [pltpu.VMEM((1, 128), i32), pltpu.SMEM((1, 128), i32), sems(1)]
    return call(public_kernel, outs, [SM, VM, VM], scratch, 10**9, 2**21, [VM, VM, SM])(distances, kept, public)


def do_spread(count, own, other):
    outs = [((count, 2) + own.shape, bf16)]
    return call(spread_kernel, outs, [VM, VM], [sems(2 * count)], 10**5, 2**20, [ANY])(own, other)[0]


def do_grads(count, grads, weight):
    return call(grads_kernel, [(grads.shape, bf16), GRID32], [VM] * 3, (), 2 * 10**9, 2**22)(count, grads, weight)


def do_weights(kept, *rest):
    outs = [KEPT16, SLAB16, KEPT32, GRID32]
    return call(weights_kernel, outs, [VM] * 5, [ROOM32, pltpu.SMEM((1, KEEP), i32), sems(1)], 3 * 10**8, 2**21)(kept, *rest)


def do_fill(listed, early):
    return call(fill_kernel, [SLAB16], [SM, VM], (), 10**6, 2**18)(listed, early)[0]


def do_near(kept, peer, kept_coeffs):
    return call(near_kernel, [KEPT16, KEPT32], [SM] + [VM] * 2, (), 10**6, 2**19)(kept, peer, kept_coeffs)


def do_far_packed(kept, listed, *rest):
    return call(far_packed_kernel, [KEPT16, KEPT32, SLAB16], [SM, SM] + [VM] * 3, (), 10**6, 2**19)(kept, listed, *rest)


def do_far_full(kept, listed, *rest):
    return call(far_full_kernel, [SLAB16, KEPT32, SLAB16], [SM, SM] + [VM] * 4, (), 10**6, 2**19)(kept, listed, *rest)


def do_base(kept, *rest):
    outs = [GRID32, ((128, 128), bf16), ((COLS, COLS), bf16)]
    return call(base_kernel, outs, [SM] + [VM] * 6, [ROOM32], 10**9, 2**22)(kept, *rest)


def do_near_last(*args):
    return call(near_last_kernel, [GRID16], [VM] * 4, (), 2 * 10**8, 2**20)(*args)[0]


def do_far_last(listed, *rest):
    return call(far_last_kernel, [GRID16], [SM] + [VM] * 5, [ROOM16], 2 * 10**8, 2**20)(listed, *rest)[0]


def swapped(block, axis, bit):
    count = lax.axis_size(axis)
    return lax.ppermute(block, axis, [(i, i ^ (1 << bit)) for i in range(count)])


def peers_list(early):
    return early[LEFT, 0, :SLABS].astype(i32)


def shards(activations, out_grads, weight, public, counts, kept, distances):
    count_x = lax.axis_size("tp") // 2
    groups = [[2 * x + z for x in range(count_x)] for z in range(2)]
    acts, grads, weight, public, kept = activations[0], out_grads[0], weight[0], public[0], kept[0, 0]

    other = swapped(acts, "tp", 0)
    public_full, early, way = do_public(distances, kept[None], public)
    early_far = swapped(early, "rep", TOP)
    other, early = lax.optimization_barrier((other, early))
    pairs = do_spread(count_x, acts, other)
    pairs, counts = lax.optimization_barrier((pairs, counts[:, None]))
    rows = lax.all_to_all(pairs, "tp", 0, 0, axis_index_groups=groups)
    turned, weight_coeffs = do_grads(counts, grads, weight)
    packed, full, kept_coeffs, moved = do_weights(kept[None], rows, turned, weight_coeffs, public_full)

    def rounds(first, second):
        def run(packed, full, early, early_far):
            if first == TOP:
                arrived = swapped(packed, "rep", first)
                if second in PACKED:
                    early, packed = lax.optimization_barrier((early, packed))
                    early_second = swapped(early, "rep", second)
                listed = peers_list(early_far)
                filled = do_fill(listed, early_far)
                if second in PACKED:
                    late, next_coeffs, peer = do_far_packed(kept, listed, arrived, filled, kept_coeffs)
                else:
                    late, next_coeffs, peer = do_far_full(kept, listed, arrived, filled, full, kept_coeffs)
            else:
                early_second = early_far
                peer = swapped(full, "rep", first)
                late, next_coeffs = do_near(kept, peer, kept_coeffs)
            arrived = swapped(late, "rep", second)
            last = do_base(kept, peer, public_full, kept_coeffs, next_coeffs, moved, weight)
            if second in PACKED:
                listed = peers_list(early_second)
                return do_far_last(listed, arrived, do_fill(listed, early_second), *last)
            return do_near_last(arrived, *last)

        return run

    ways = [(bit, TOP) for bit in range(TOP)] + [(TOP, bit) for bit in range(TOP)]
    return lax.switch(way[0], [rounds(*pair) for pair in ways], packed, full, early, early_far)[None]


def solution(mesh):
    return jax.shard_map(
        shards,
        mesh=mesh,
        in_specs=(
            P("rep", "tp", None),
            P("rep", None, "tp"),
            P("rep", None, "tp"),
            P("rep", None, "tp"),
            P("rep"),
            P("rep", "tp", None),
            P(),
        ),
        out_specs=P("rep", None, "tp"),
        check_vma=False,
    )
```

```python
import jax
import jax.numpy as jnp
import numpy as np
from jax import lax
from jax.experimental import pallas as pl
from jax.experimental.pallas import tpu as pltpu
from jax.sharding import PartitionSpec as P


learn_rate = 0.02
step = 0.25
ROWS, COLS, KEEP, SLABS, TOP = 256, 512, 40, 64, 5
LEFT = SLABS - KEEP
PACKED = (1, 2, 3, 4, TOP)
f32, bf16, i32 = jnp.float32, jnp.bfloat16, jnp.int32
VM = pl.BlockSpec(memory_space=pltpu.VMEM)
SM = pl.BlockSpec(memory_space=pltpu.SMEM)


def cosines(freq, place):
    phase = ((2 * place + 1) * freq) & 255
    scale = jnp.where(freq == 0, np.float32(np.sqrt(1 / 64)), np.float32(np.sqrt(2 / 64)))
    return scale * jnp.cos(phase.astype(f32) * np.float32(np.pi / 128))


def lines(shape, axis):
    return lax.broadcasted_iota(i32, shape, axis)


def spectrum():
    shape = (64, 128)
    return cosines(lines(shape, 0), lines(shape, 1) & 63)


def left_table(table):
    groups = [table[8 * ub : 8 * ub + 8] for ub in range(8) for _ in range(2)]
    shape = (128, 128)
    return jnp.where((lines(shape, 0) >> 3) & 1 == lines(shape, 1) >> 6, jnp.concatenate(groups, 0), 0.0)


def left_table_t():
    shape = (64, 128)
    r = lines(shape, 1)
    part = cosines((r >> 4) * 8 + (r & 7), lines(shape, 0))
    odd = (r >> 3) & 1
    return jnp.concatenate([jnp.where(odd == 0, part, 0.0), jnp.where(odd == 1, part, 0.0)], 0)


def right_table():
    shape = (64, COLS)
    j = lines(shape, 1)
    part = cosines((j >> 6) * 8 + (j & 7), lines(shape, 0))
    tile = (j >> 3) & 7
    return jnp.concatenate([jnp.where(tile == b, part, 0.0).astype(bf16) for b in range(8)], 0)


def right_table_t():
    table = spectrum()
    low = lines(table.shape, 1) < 64
    masked = jnp.where(low, table, 0.0), jnp.where(low, 0.0, table)
    zeros = jnp.zeros((8, 128), f32)
    columns = []
    for c in range(4):
        groups = [masked[b & 1][8 * vb : 8 * vb + 8] if b >> 1 == c else zeros for vb in range(8) for b in range(8)]
        columns.append(jnp.concatenate(groups, 0))
    return jnp.concatenate(columns, 1)


def dot(a, b):
    return jnp.dot(a, b, preferred_element_type=f32)


def split(x):
    high = x.astype(bf16)
    return high, (x - high.astype(f32)).astype(bf16)


def by_halves(run, x):
    return jnp.concatenate([run(x[:128]), run(x[128:])], 0)


def left_dot(table, x):
    high, low = split(x)
    return dot(table[0], high) + (dot(table[0], low) + dot(table[1], high))


def right_dot(x, table):
    high, low = split(x)
    return dot(high, table[0]) + (dot(low, table[0]) + dot(high, table[1]))


def low_lanes():
    return lax.broadcasted_iota(i32, (128, 128), 1) < 64


def to_slabs(grid, put):
    low = low_lanes()
    for q in range(4):
        top = grid[:128, 128 * q : 128 * (q + 1)]
        bottom = grid[128:, 128 * q : 128 * (q + 1)]
        even = jnp.where(low, top, pltpu.roll(bottom, 64, 1))
        odd = jnp.where(low, pltpu.roll(top, 64, 1), bottom)
        for ub in range(8):
            put(ub * 8 + 2 * q, even[16 * ub : 16 * (ub + 1)])
            put(ub * 8 + 2 * q + 1, odd[16 * ub : 16 * (ub + 1)])


def from_slabs(get):
    low = low_lanes()
    tops, bottoms = [], []
    for q in range(4):
        even = jnp.concatenate([get(ub * 8 + 2 * q) for ub in range(8)], 0)
        odd = jnp.concatenate([get(ub * 8 + 2 * q + 1) for ub in range(8)], 0)
        tops.append(jnp.where(low, even, pltpu.roll(odd, 64, 1)))
        bottoms.append(jnp.where(low, pltpu.roll(even, 64, 1), odd))
    return jnp.concatenate([jnp.concatenate(tops, 1), jnp.concatenate(bottoms, 1)], 0)


def list_all(kept, room):
    room[...] = jnp.full((1, 128), -1, i32)
    room[:, :KEEP] = kept[...]
    named = room[...]
    shape = (SLABS, 128)
    s, lane = lines(shape, 0), lines(shape, 1)
    hits = jnp.where(s == named, 1.0, 0.0)
    free = jnp.broadcast_to(1.0 - jnp.max(hits, axis=1, keepdims=True), shape)
    shape = (SLABS, SLABS)
    below = jnp.where(lines(shape, 1) < lines(shape, 0), 1.0, 0.0)
    rank = dot(below.astype(bf16), free.astype(bf16))
    here = jnp.where((lane - KEEP).astype(f32) == rank, free, 0.0)
    rest = jnp.sum(here * s.astype(f32), axis=0, keepdims=True)
    row = jnp.where(lane[:1] < KEEP, named.astype(f32), rest)
    room[...] = row.astype(i32)
    return row


def find_way(distances, way):
    sizes = [sum((distances[0, k] > 1 << bit).astype(i32) for bit in range(TOP)) for k in range(2)]
    way[0] = jnp.where(sizes[1] == TOP, sizes[0], TOP + sizes[1])


def public_kernel(distances_row, kept, public, full, early, way, room, listed, distances, sem):
    to_distances = pltpu.make_async_copy(distances_row, distances, sem.at[1])
    to_distances.start()
    row = list_all(kept, room)
    to_scalars = pltpu.make_async_copy(room, listed, sem.at[0])
    to_scalars.start()
    left, right = left_table(spectrum()).astype(bf16), right_table()
    grid = by_halves(lambda x: dot(left, x), dot(public[...], right).astype(bf16))

    def put(s, slab):
        full[s] = slab.astype(bf16)

    to_slabs(grid, put)
    early[LEFT] = jnp.broadcast_to(row, (16, 128)).astype(bf16)
    to_scalars.wait()
    for j in range(LEFT):
        early[j] = full[listed[0, KEEP + j]]
    to_distances.wait()
    find_way(distances, way)


def spread_kernel(own, other, out, sems):
    copies = []
    for x in range(out.shape[0]):
        for k, part in enumerate((own, other)):
            copies.append(pltpu.make_async_copy(part, out.at[x, k], sems.at[2 * x + k]))
    for copy in copies:
        copy.start()
    for copy in copies:
        copy.wait()


def own_place():
    return lax.axis_index("tp") & 1


def grads_kernel(count, grads, weight, turned, weight_coeffs):
    place = own_place()
    right = right_table()
    part = grads.shape[0] // 4
    for k in range(4):
        y = dot(grads[k * part : (k + 1) * part], right)
        token = k * part + lines((part, COLS), 0)
        y = jnp.where(token < count[...], y, 0.0).astype(bf16)
        for z in range(2):
            to = k * part + ((z + place) & 1) * (part // 2)
            turned[pl.ds(pl.multiple_of(to, part // 2), part // 2), :] = y[part // 2 * z : part // 2 * (z + 1)]
    left = left_table(spectrum()).astype(bf16)
    weight_coeffs[...] = by_halves(lambda x: dot(left, x), dot(weight[...], right).astype(bf16))


def weights_kernel(kept_row, acts, turned, weight_coeffs, public_full, packed, full, kept_coeffs, moved, slabs, kept, sem):
    to_scalars = pltpu.make_async_copy(kept_row, kept, sem.at[0])
    to_scalars.start()
    left = split(left_table(spectrum()))
    dims = (((1,), (1,)), ((), ()))
    x = acts[...].reshape(-1, ROWS)
    rows = []
    for h in range(2):
        half = x[:, 128 * h : 128 * (h + 1)]
        row = lax.dot_general(left[0], half, dims, preferred_element_type=f32)
        rows.append((row + lax.dot_general(left[1], half, dims, preferred_element_type=f32)).astype(bf16))
    change = -learn_rate * dot(jnp.concatenate(rows, 0), turned[...])
    moved[...] = change

    def put(s, slab):
        slabs[s] = slab

    to_slabs(weight_coeffs[...] + change, put)
    full[...] = public_full[...]
    to_scalars.wait()
    for i in range(KEEP):
        s = kept[0, i]
        slab = slabs[s]
        short = slab.astype(bf16)
        kept_coeffs[i] = slab
        packed[i] = short
        full[s] = short


def fill_kernel(listed, early, peer):
    for j in range(LEFT):
        peer[listed[KEEP + j]] = early[j]
    for i in range(KEEP):
        peer[listed[i]] = jnp.zeros((16, 128), bf16)


def mix(kept, peer, kept_coeffs, next_coeffs, put):
    for i in range(KEEP):
        s = kept[i]
        value = kept_coeffs[i]
        value = value + step * (peer[s].astype(f32) - value)
        next_coeffs[i] = value
        put(i, s, value.astype(bf16))


def mix_packed(kept, peer, kept_coeffs, packed, next_coeffs):
    def put(i, s, slab):
        packed[i] = slab

    mix(kept, peer, kept_coeffs, next_coeffs, put)


def near_kernel(kept, peer, kept_coeffs, packed, next_coeffs):
    mix_packed(kept, peer, kept_coeffs, packed, next_coeffs)


def unpack(listed, arrived, filled, peer):
    peer[...] = filled[...]
    for i in range(KEEP):
        peer[listed[i]] = arrived[i]


def far_packed_kernel(kept, listed, arrived, filled, kept_coeffs, packed, next_coeffs, peer):
    unpack(listed, arrived, filled, peer)
    mix_packed(kept, peer, kept_coeffs, packed, next_coeffs)


def far_full_kernel(kept, listed, arrived, filled, own, kept_coeffs, full, next_coeffs, peer):
    unpack(listed, arrived, filled, peer)
    full[...] = own[...]

    def put(i, s, slab):
        full[s] = slab

    mix(kept, peer, kept_coeffs, next_coeffs, put)


def base_kernel(kept, peer, public_full, kept_coeffs, next_coeffs, moved, weight, out, left_high, right_high, delta):
    delta[...] = step * peer[...].astype(f32) - 2 * step * public_full[...].astype(f32)
    for i in range(KEEP):
        s = kept[i]
        delta[s] = step * (peer[s].astype(f32) - kept_coeffs[i] - next_coeffs[i])
    grid = from_slabs(lambda s: delta[s]) + moved[...]
    left, right = split(left_table_t()), split(right_table_t())
    left_high[...] = left[0]
    right_high[...] = right[0]
    out[...] = weight[...].astype(f32) + by_halves(lambda x: left_dot(left, x), right_dot(grid, right))


def finish(get, base, left_t, right_t, out):
    grid = (step * from_slabs(lambda s: get(s).astype(f32))).astype(bf16)
    turned = dot(grid, right_t[...]).astype(bf16)
    out[...] = (base[...] + by_halves(lambda x: dot(left_t[...], x), turned)).astype(bf16)


def near_last_kernel(peer, base, left_t, right_t, out):
    finish(lambda s: peer[s], base, left_t, right_t, out)


def far_last_kernel(listed, arrived, filled, base, left_t, right_t, out, slabs):
    unpack(listed, arrived, filled, slabs)
    finish(lambda s: slabs[s], base, left_t, right_t, out)


def call(kernel, outs, specs, scratch=(), flops=0, moves=0, out_specs=None):
    return pl.pallas_call(
        kernel,
        out_shape=[jax.ShapeDtypeStruct(shape, kind) for shape, kind in outs],
        in_specs=specs,
        out_specs=out_specs or [VM] * len(outs),
        scratch_shapes=list(scratch),
        compiler_params=pltpu.CompilerParams(vmem_limit_bytes=16 * 2**20),
        cost_estimate=pl.CostEstimate(flops=flops, bytes_accessed=moves, transcendentals=0),
    )


SLAB16 = ((SLABS, 16, 128), bf16)
KEPT32 = ((KEEP, 16, 128), f32)
KEPT16 = ((KEEP, 16, 128), bf16)
GRID32 = ((ROWS, COLS), f32)
GRID16 = ((ROWS, COLS), bf16)
REST = pltpu.SMEM((SLABS + 1,), i32)
ROOM32, ROOM16 = pltpu.VMEM((SLABS, 16, 128), f32), pltpu.VMEM((SLABS, 16, 128), bf16)


ANY = pl.BlockSpec(memory_space=pl.ANY)


def sems(count):
    return pltpu.SemaphoreType.DMA((count,))


def do_public(distances, kept, public):
    outs = [SLAB16, ((LEFT + 1, 16, 128), bf16), ((1,), i32)]
    scratch = [pltpu.VMEM((1, 128), i32), pltpu.SMEM((1, 128), i32), pltpu.SMEM((1, 2), i32), sems(2)]
    return call(public_kernel, outs, [VM, VM, VM], scratch, 10**9, 2**21, [VM, VM, SM])(distances, kept, public)


def do_spread(count, own, other):
    outs = [((count, 2) + own.shape, bf16)]
    return call(spread_kernel, outs, [VM, VM], [sems(2 * count)], 10**5, 2**20, [ANY])(own, other)[0]


def do_grads(count, grads, weight):
    return call(grads_kernel, [(grads.shape, bf16), GRID32], [VM] * 3, (), 2 * 10**9, 2**22)(count, grads, weight)


def do_weights(kept, *rest):
    outs = [KEPT16, SLAB16, KEPT32, GRID32]
    return call(weights_kernel, outs, [VM] * 5, [ROOM32, pltpu.SMEM((1, KEEP), i32), sems(1)], 3 * 10**8, 2**21)(kept, *rest)


def do_fill(listed, early):
    return call(fill_kernel, [SLAB16], [SM, VM], (), 10**6, 2**18)(listed, early)[0]


def do_near(kept, peer, kept_coeffs):
    return call(near_kernel, [KEPT16, KEPT32], [SM] + [VM] * 2, (), 10**6, 2**19)(kept, peer, kept_coeffs)


def do_far_packed(kept, listed, *rest):
    return call(far_packed_kernel, [KEPT16, KEPT32, SLAB16], [SM, SM] + [VM] * 3, (), 10**6, 2**19)(kept, listed, *rest)


def do_far_full(kept, listed, *rest):
    return call(far_full_kernel, [SLAB16, KEPT32, SLAB16], [SM, SM] + [VM] * 4, (), 10**6, 2**19)(kept, listed, *rest)


def do_base(kept, *rest):
    outs = [GRID32, ((128, 128), bf16), ((COLS, COLS), bf16)]
    return call(base_kernel, outs, [SM] + [VM] * 6, [ROOM32], 10**9, 2**22)(kept, *rest)


def do_near_last(*args):
    return call(near_last_kernel, [GRID16], [VM] * 4, (), 2 * 10**8, 2**20)(*args)[0]


def do_far_last(listed, *rest):
    return call(far_last_kernel, [GRID16], [SM] + [VM] * 5, [ROOM16], 2 * 10**8, 2**20)(listed, *rest)[0]


def swapped(block, axis, bit):
    count = lax.axis_size(axis)
    return lax.ppermute(block, axis, [(i, i ^ (1 << bit)) for i in range(count)])


def peers_list(early):
    return early[LEFT, 0, :SLABS].astype(i32)


def shards(activations, out_grads, weight, public, counts, kept, distances):
    count_x = lax.axis_size("tp") // 2
    groups = [[2 * x + z for x in range(count_x)] for z in range(2)]
    acts, grads, weight, public, kept = activations[0], out_grads[0], weight[0], public[0], kept[0, 0]

    other = swapped(acts, "tp", 0)
    public_full, early, way = do_public(distances[None], kept[None], public)
    early_far = swapped(early, "rep", TOP)
    other, early = lax.optimization_barrier((other, early))
    pairs = do_spread(count_x, acts, other)
    pairs, counts = lax.optimization_barrier((pairs, counts[:, None]))
    rows = lax.all_to_all(pairs, "tp", 0, 0, axis_index_groups=groups)
    turned, weight_coeffs = do_grads(counts, grads, weight)
    packed, full, kept_coeffs, moved = do_weights(kept[None], rows, turned, weight_coeffs, public_full)

    def rounds(first, second):
        def run(packed, full, early, early_far):
            if first == TOP:
                arrived = swapped(packed, "rep", first)
                if second in PACKED:
                    early, packed = lax.optimization_barrier((early, packed))
                    early_second = swapped(early, "rep", second)
                listed = peers_list(early_far)
                filled = do_fill(listed, early_far)
                if second in PACKED:
                    late, next_coeffs, peer = do_far_packed(kept, listed, arrived, filled, kept_coeffs)
                else:
                    late, next_coeffs, peer = do_far_full(kept, listed, arrived, filled, full, kept_coeffs)
            else:
                early_second = early_far
                peer = swapped(full, "rep", first)
                late, next_coeffs = do_near(kept, peer, kept_coeffs)
            arrived = swapped(late, "rep", second)
            last = do_base(kept, peer, public_full, kept_coeffs, next_coeffs, moved, weight)
            if second in PACKED:
                listed = peers_list(early_second)
                return do_far_last(listed, arrived, do_fill(listed, early_second), *last)
            return do_near_last(arrived, *last)

        return run

    ways = [(bit, TOP) for bit in range(TOP)] + [(TOP, bit) for bit in range(TOP)]
    return lax.switch(way[0], [rounds(*pair) for pair in ways], packed, full, early, early_far)[None]


def solution(mesh):
    return jax.shard_map(
        shards,
        mesh=mesh,
        in_specs=(
            P("rep", "tp", None),
            P("rep", None, "tp"),
            P("rep", None, "tp"),
            P("rep", None, "tp"),
            P("rep"),
            P("rep", "tp", None),
            P(),
        ),
        out_specs=P("rep", None, "tp"),
        check_vma=False,
    )
```
